256 devices in a mesh: grp: 32 (over z_hi, y, x), tp: 8 (over z_lo, core).
Axes of the slice: x: 4, y: 4, z: 8 (z_hi: 2, z_lo: 4; z = z_hi * 4 + z_lo), core: 2. Of those that a mesh axis runs over, the one named last changes fastest.
Arguments:
- tokens: bfloat16 [512, 16384], P('grp', 'tp'), may hold values from -54 to 54
- queries: bfloat16 [512, 8192], P('grp', 'tp'), may hold values from -5 to 5
- new_key: bfloat16 [512, 1024], P('grp', 'tp'), may hold values from -5 to 5
- new_value: bfloat16 [512, 1024], P('grp', 'tp'), may hold values from -4 to 4
- key_cache: bfloat16 [512, 48, 1024], P('grp', None, 'tp'), may hold values from -5 to 5
- value_cache: bfloat16 [512, 48, 1024], P('grp', None, 'tp'), may hold values from -4 to 4
- lengths: int32 [512], P('grp'), may hold values from 1 to 48
- group_of: int32 [512], replicated, may hold values from 0 to 31, as said below
- out_weight: bfloat16 [8192, 16384], P('tp', 'grp'), may hold values from -0.0625 to 0.0625
- norm_gain: bfloat16 [16384], P('tp'), may hold values from 0.5 to 1.5
- gate_weight: bfloat16 [16384, 26624], P('tp', 'grp'), may hold values from -0.046875 to 0.046875
- up_weight: bfloat16 [16384, 26624], P('tp', 'grp'), may hold values from -0.046875 to 0.046875
- down_weight: bfloat16 [26624, 16384], P('grp', 'tp'), may hold values from -0.0390625 to 0.0390625
Outputs:
- layer_out: bfloat16 [512, 16384], P('grp', 'tp')
The draws below stay inside these ranges and needn't reach their ends.
Inputs may be any that keep to these rules, and one draw needn't show every extreme that they name: `group_of`: the 16 rows of one device name any group at most 2 times and some group exactly 2 times; every group is named by exactly 16 rows.
All inputs are finite; a program needn't handle non-finite values.
Results may differ from the reference program's by a relative error of at most 0.012.
Values may be sent and summed in bfloat16 or wider, within the bound.
No kernel may reach another device: no remote copies, remote signals or barrier semaphores. Data moves between devices by JAX's collectives and lax.ppermute only.
A program may use at most 64 MiB of HBM per device.

```python
import math
import jax
import jax.numpy as jnp
from jax import lax

D = 16384
FFW = 26624
HQ = 64
KVH = 8
HD = 128
MAXLEN = 48
ROWS_DEV = 16
ROWS = 512
CAP = 2
N_GRP = 32


def assignment(key):
    key = jax.random.fold_in(key, 101)
    first, second, third = jax.random.split(key, 3)
    shifts = jax.random.permutation(first, N_GRP)
    offsets = jax.random.permutation(second, N_GRP)[jnp.arange(ROWS_DEV) // CAP]
    orders = jax.vmap(lambda sub_key: jax.random.permutation(sub_key, ROWS_DEV))(jax.random.split(third, N_GRP))
    targets = (shifts[:, None] + offsets[orders]) % N_GRP
    group_of = targets.reshape(ROWS).astype(jnp.int32)
    return group_of


def draw_group_of(key, part):
    group_of = assignment(key)
    return group_of


def draw_lengths(key, part):
    key = jax.random.fold_in(key, 17)
    first, second, third = jax.random.split(key, 3)
    levels = jnp.left_shift(1, jax.random.randint(first, (N_GRP,), 0, 4))
    reaches = jnp.maximum(MAXLEN * levels // 8, 1)
    reaches = jnp.repeat(reaches, ROWS_DEV)
    raw_draws = jax.random.randint(second, (ROWS,), 0, MAXLEN)
    lengths = 1 + raw_draws % reaches
    peak_row = jax.random.randint(third, (), 0, ROWS)
    return jnp.where(jnp.arange(ROWS) == peak_row, MAXLEN, lengths).astype(jnp.int32)


def draw_tokens(key, part):
    key = jax.random.fold_in(key, 5)
    first, second = jax.random.split(key)
    columns = jnp.power(10.0, jnp.arange(D, dtype=jnp.float32) / D - 0.5)
    row_scale = jnp.power(10.0, jax.random.uniform(first, (ROWS, 1), minval=-0.5, maxval=0.5))
    base_vals = jax.random.truncated_normal(second, -3.0, 3.0, (ROWS, D))
    return (base_vals * row_scale * columns[None, :]).astype(jnp.bfloat16)


def draw_queries(key, part):
    own_key = jax.random.fold_in(key, 11)
    return jax.random.truncated_normal(own_key, -4.0, 4.0, (ROWS, HQ * HD)).astype(jnp.bfloat16)


def draw_new_key(key, part):
    own_key = jax.random.fold_in(key, 23)
    return jax.random.truncated_normal(own_key, -4.0, 4.0, (ROWS, KVH * HD)).astype(jnp.bfloat16)


def draw_key_cache(key, part):
    own_key = jax.random.fold_in(key, 31)
    return jax.random.truncated_normal(own_key, -4.0, 4.0, (ROWS, MAXLEN, KVH * HD)).astype(jnp.bfloat16)


def shard_levels(key, extent, shards, low, high):
    level = 1.0
    for dim, shards_of in shards:
        draws = jax.random.uniform(jax.random.fold_in(jax.random.fold_in(key, 6), dim), (shards_of,), jnp.float32, low / len(shards), high / len(shards))
        level = level * jnp.repeat(jnp.exp(draws), extent[dim] // shards_of).reshape((-1,) + (1,) * (len(extent) - 1 - dim))
    return level


def centred(stream_key, extent, deviation, limit, pieces=(), held_as=jnp.bfloat16):
    result = deviation * jax.random.normal(stream_key, extent, jnp.float32)
    if pieces:
        result = result * shard_levels(stream_key, extent, pieces, -0.22, 0.18)
    return jnp.clip(result, -limit, limit).astype(held_as)


def setup_inputs(seed: int = 0) -> dict:
    seeds = jax.random.split(jax.random.key(seed), 14)
    return {
        "tokens": draw_tokens(jax.random.fold_in(seeds[13], 71), 0),
        "queries": draw_queries(jax.random.fold_in(seeds[13], 71), 0),
        "new_key": draw_new_key(jax.random.fold_in(seeds[13], 71), 0),
        "new_value": centred(seeds[3], (ROWS, KVH * HD), 1.0, 4.0, ((0, 32), (1, 8))),
        "key_cache": draw_key_cache(jax.random.fold_in(seeds[13], 71), 0),
        "value_cache": centred(seeds[5], (ROWS, MAXLEN, KVH * HD), 1.0, 4.0, ((0, 32), (2, 8))),
        "lengths": draw_lengths(jax.random.fold_in(seeds[13], 71), 0),
        "group_of": draw_group_of(jax.random.fold_in(seeds[13], 71), 0),
        "out_weight": centred(seeds[8], (HQ * HD, D), (HQ * HD) ** -0.5, 0.0625, ((0, 8), (1, 32))),
        "norm_gain": jnp.clip(1.0 + 0.1 * jax.random.normal(seeds[9], (D,), jnp.float32), 0.5, 1.5).astype(jnp.bfloat16),
        "gate_weight": centred(seeds[10], (D, FFW), D ** -0.5, 0.046875, ((0, 8), (1, 32))),
        "up_weight": centred(seeds[11], (D, FFW), D ** -0.5, 0.046875, ((0, 8), (1, 32))),
        "down_weight": centred(seeds[12], (FFW, D), FFW ** -0.5, 0.0390625, ((0, 32), (1, 8))),
    }


def row_positions(group_of):
    onehot = (group_of[:, None] == jnp.arange(N_GRP, dtype=jnp.int32)[None, :]).astype(jnp.int32)
    earlier = jnp.cumsum(onehot, axis=0) - onehot
    return (group_of * ROWS_DEV + lax.optimization_barrier(jnp.sum(earlier * onehot, axis=1))).astype(jnp.int32)

def reference(tokens, queries, new_key, new_value, key_cache, value_cache, lengths, group_of, out_weight, norm_gain, gate_weight, up_weight, down_weight):
    position = row_positions(group_of)
    inverse = jnp.zeros((ROWS,), jnp.int32).at[position].set(jnp.arange(ROWS, dtype=jnp.int32))
    per_kv = HQ // KVH
    query_view = queries[inverse].astype(jnp.float32).reshape(ROWS, KVH, per_kv, HD)
    key_new = new_key[inverse].astype(jnp.float32).reshape(ROWS, KVH, HD)
    value_new = new_value[inverse].astype(jnp.float32).reshape(ROWS, KVH, HD)
    key_view = key_cache.astype(jnp.float32).reshape(ROWS, MAXLEN, KVH, HD)
    value_view = value_cache.astype(jnp.float32).reshape(ROWS, MAXLEN, KVH, HD)
    qk_scale = 1.0 / math.sqrt(HD)
    scores = jnp.einsum('rkjd,rlkd->rkjl', query_view, key_view) * qk_scale
    own_score = jnp.einsum('rkjd,rkd->rkj', query_view, key_new) * qk_scale
    live_mask = (jnp.arange(MAXLEN, dtype=jnp.int32)[None, :] < lengths[:, None])[:, None, None, :]
    masked = jnp.where(live_mask, scores, -1e+30)
    row_top = jnp.maximum(lax.optimization_barrier(jnp.max(masked, axis=3)), own_score)
    exp_live = jnp.exp(masked - row_top[..., None])
    exp_own = jnp.exp(own_score - row_top)
    totals = lax.optimization_barrier(jnp.sum(exp_live, axis=3)) + exp_own
    weights = (exp_live / totals[..., None]).astype(jnp.bfloat16)
    own_weight = (exp_own / totals).astype(jnp.bfloat16)
    head_out = jnp.einsum('rkjl,rlkd->rkjd', weights.astype(jnp.float32), value_view)
    head_out = head_out + own_weight.astype(jnp.float32)[..., None] * value_new[:, :, None, :]
    head_out = head_out.astype(jnp.bfloat16).reshape(ROWS, HQ * HD)
    attn_out = jnp.dot(head_out[position], out_weight, preferred_element_type=jnp.float32).astype(jnp.bfloat16)
    residual = (tokens.astype(jnp.float32) + attn_out.astype(jnp.float32)).astype(jnp.bfloat16)
    wide = residual.astype(jnp.float32)
    normed = wide * lax.rsqrt(lax.optimization_barrier(jnp.mean(wide * wide, axis=1, keepdims=True)) + 1e-05) * norm_gain.astype(jnp.float32)[None, :]
    normed = normed.astype(jnp.bfloat16)
    width = FFW // 8

    def ffn_block(running, block_index):
        begin = block_index * width
        gate_part = jnp.dot(normed, lax.dynamic_slice_in_dim(gate_weight, begin, width, 1), preferred_element_type=jnp.float32)
        up_part = jnp.dot(normed, lax.dynamic_slice_in_dim(up_weight, begin, width, 1), preferred_element_type=jnp.float32)
        hidden = (jax.nn.silu(gate_part) * up_part).astype(jnp.bfloat16)
        down_part = lax.dynamic_slice_in_dim(down_weight, begin, width, 0)
        return (running + jnp.dot(hidden, down_part, preferred_element_type=jnp.float32), None)
    running, unused = lax.scan(ffn_block, jnp.zeros((ROWS, D), jnp.float32), jnp.arange(8, dtype=jnp.int32))
    return (wide + running).astype(jnp.bfloat16)
```

```python
import functools
import math

import jax
import jax.numpy as jnp
import numpy as np
from jax import lax
from jax.experimental import pallas as pl
from jax.experimental.pallas import tpu as pltpu
from jax.sharding import Mesh
from jax.sharding import PartitionSpec as P

D = 16384
HD = 128
AXES = ("z_hi", "y", "x", "z_lo", "core")
SIZES = (2, 4, 4, 4, 2)
GRP = ("z_hi", "y", "x")
TP = ("z_lo", "core")
YX = ("y", "x")
BF = jnp.bfloat16
F32 = jnp.float32
MIB = 1 << 20
PAD = 896


def flat(z_hi, y, x, z_lo, core):
    return (((z_hi * 4 + y) * 4 + x) * 4 + z_lo) * 2 + core


def spread_pairs(flip):
    pairs = []
    for z_hi in range(2):
        for y in range(4):
            for x in range(4):
                for z_lo in range(4):
                    for core in range(2):
                        src = flat(z_hi, y, x, z_lo, core)
                        dst = flat(core ^ flip, z_lo, x, 2 * z_hi + y // 2, y % 2)
                        pairs.append((src, dst))
    return pairs


def swap(v, axis):
    return lax.ppermute(v, axis, [(0, 1), (1, 0)])


def pick(v, index):
    return lax.dynamic_index_in_dim(v, index, 0, keepdims=False)


def spread(v, axes, count):
    copies = jnp.broadcast_to(v[None], (count,) + v.shape)
    return lax.all_to_all(copies, axes, split_axis=0, concat_axis=0, tiled=True)


def call(body, out_shape, *operands, scalars=(), scratch=(), limit=24, flops=0, moved=0):
    whole = pl.BlockSpec(memory_space=pltpu.VMEM)
    single = not isinstance(out_shape, (list, tuple))
    specs = [pl.BlockSpec(memory_space=pltpu.SMEM)] * len(scalars) + [whole] * len(operands)
    return pl.pallas_call(
        body,
        out_shape=out_shape,
        in_specs=specs,
        out_specs=whole if single else [whole] * len(out_shape),
        scratch_shapes=list(scratch),
        compiler_params=pltpu.CompilerParams(vmem_limit_bytes=limit * MIB),
        cost_estimate=pl.CostEstimate(flops=flops, bytes_accessed=moved, transcendentals=0),
    )(*[jnp.reshape(s, (1,)).astype(jnp.int32) for s in scalars], *operands)


def shape(dims, dtype):
    return jax.ShapeDtypeStruct(dims, dtype)


def dot(a, b):
    return jnp.dot(a, b, preferred_element_type=F32)


def attend_body(rows, cache_len, heads, slot_ref, got_ref, key_ref, value_ref, len_ref, out_ref):
    slots = lax.broadcasted_iota(jnp.int32, (rows, got_ref.shape[0]), 1)
    compact = (slot_ref[...] == slots).astype(F32).astype(BF)
    arrived = dot(compact, got_ref[...])
    q_cols = heads * HD
    rounded = arrived[:, :q_cols].astype(BF)
    tall = jnp.concatenate([rounded[:, j * HD : (j + 1) * HD] for j in range(heads)], axis=0)
    key_new = jnp.concatenate([arrived[:, q_cols : q_cols + HD]] * heads, axis=0)
    value_new = jnp.concatenate([arrived[:, q_cols + HD :]] * heads, axis=0)
    scale = 1.0 / math.sqrt(HD)
    scores = lax.dot_general(tall, key_ref[...], (((1,), (1,)), ((), ())), preferred_element_type=F32) * scale
    own = jnp.sum(tall.astype(F32) * key_new, axis=1, keepdims=True) * scale
    spot = lax.broadcasted_iota(jnp.int32, scores.shape, 1)
    row = lax.rem(lax.broadcasted_iota(jnp.int32, scores.shape, 0), rows)
    start = row * cache_len
    lens = jnp.concatenate([len_ref[...]] * heads, axis=0)
    live = (spot >= start) & (spot < start + lens)
    masked = jnp.where(live, scores, -1e30)
    top = jnp.maximum(jnp.max(masked, axis=1, keepdims=True), own)
    exp_live = jnp.where(live, jnp.exp(masked - top), 0.0)
    exp_own = jnp.exp(own - top)
    total = jnp.sum(exp_live, axis=1, keepdims=True) + exp_own
    weights = (exp_live / total).astype(BF)
    own_weight = (exp_own / total).astype(BF).astype(F32)
    out = (dot(weights, value_ref[...]) + own_weight * value_new).astype(BF)
    for j in range(heads):
        out_ref[:, j * HD : (j + 1) * HD] = out[j * rows : (j + 1) * rows]


def project_body(send_pos, keep_pos, heads_ref, weight_ref, send_ref, keep_ref):
    product = dot(heads_ref[...], weight_ref[...]).astype(BF)
    for pos, out in ((send_pos, send_ref), (keep_pos, keep_ref)):
        spot = lax.broadcasted_iota(jnp.int32, (pos.shape[0], product.shape[0]), 1)
        unsort = (pos[...] == spot).astype(F32).astype(BF)
        out[...] = dot(unsort, product).astype(BF)


def split_body(z_lo, keep_ref, got_ref, own_ref, one_ref, two_ref, three_ref):
    rows = own_ref.shape[0]
    for step, out in enumerate((own_ref, one_ref, two_ref, three_ref)):
        at = pl.ds(pl.multiple_of((z_lo[0] ^ step) * rows, rows), rows)
        out[...] = (keep_ref[at, :].astype(F32) + got_ref[at, :].astype(F32)).astype(out.dtype)


def line_reduce(keep, got, z_lo):
    rows, cols = keep.shape[0] // 4, keep.shape[1]
    outs = [shape((rows, cols), F32)] + [shape((rows, cols), BF)] * 3
    own, *pieces = call(split_body, outs, keep, got, scalars=(z_lo,))
    return [own] + [
        lax.ppermute(piece, "z_lo", [(i, i ^ step) for i in range(4)])
        for step, piece in zip((1, 2, 3), pieces)
    ]


def gate_up_body(core, rows_ref, gain_ref, gate_ref, up_ref, send_ref, keep_ref, total):
    planes, blocks, count, cols = rows_ref.shape
    hid = gate_ref.shape[1]
    rows = planes * count
    squares = jnp.zeros((rows, 1), F32)
    parts = []
    for b in range(blocks):
        wide = rows_ref[:, b].reshape(rows, cols).astype(F32)
        squares += jnp.sum(wide * wide, axis=1, keepdims=True)
        parts.append((wide * gain_ref[:, b * cols : (b + 1) * cols].astype(F32)).astype(BF))
    scaled = jnp.concatenate(parts, axis=1)
    total[:, :hid] = dot(scaled, gate_ref[...])
    total[:, PAD : PAD + hid] = dot(scaled, up_ref[...])
    high = squares.astype(BF).astype(F32)
    lane = lax.broadcasted_iota(jnp.int32, (rows, PAD - hid), 1)
    total[:, hid:PAD] = jnp.where(lane == 0, high, jnp.where(lane == 1, squares - high, 0.0))
    half = rows // 2
    send_ref[...] = total[pl.ds(pl.multiple_of((1 - core[0]) * half, half), half), :].astype(BF)
    keep_ref[...] = total[pl.ds(pl.multiple_of(core[0] * half, half), half), :]


def hidden_body(own_ref, one_ref, two_ref, three_ref, out_ref):
    hid = out_ref.shape[1]
    sums = own_ref[...] + one_ref[...].astype(F32) + two_ref[...].astype(F32) + three_ref[...].astype(F32)
    mean_square = (sums[:, hid : hid + 1] + sums[:, hid + 1 : hid + 2]) / D
    inv = lax.rsqrt(mean_square + 1e-05)
    gate = sums[:, :hid] * inv
    up = sums[:, PAD : PAD + hid] * inv
    out_ref[...] = (gate / (1.0 + jnp.exp(-gate)) * up).astype(BF)


def join_body(z_lo, own_ref, one_ref, two_ref, three_ref, out_ref):
    rows = own_ref.shape[0]
    for step, piece in enumerate((own_ref, one_ref, two_ref, three_ref)):
        out_ref[pl.ds(pl.multiple_of((z_lo[0] ^ step) * rows, rows), rows), :] = piece[...]


def down_body(core, own_ref, other_ref, weight_ref, out_ref):
    half = own_ref.shape[0]
    out_ref[pl.ds(pl.multiple_of(core[0] * half, half), half), :] = dot(own_ref[...], weight_ref[...]).astype(BF)
    out_ref[pl.ds(pl.multiple_of((1 - core[0]) * half, half), half), :] = dot(
        other_ref[...], weight_ref[...]
    ).astype(BF)


def feed_forward(gathered, gain, gate_weight, up_weight, down_weight, core, z_lo):
    rows = gathered.shape[0] * gathered.shape[2]
    hid, width = down_weight.shape
    cols = PAD + hid
    outs = [shape((rows // 2, cols), BF), shape((rows // 2, cols), F32)]
    send, keep = call(
        gate_up_body, outs, gathered, gain, gate_weight, up_weight,
        scalars=(core,), scratch=[pltpu.VMEM((rows, cols), F32)], limit=32, flops=4 * rows * width * hid,
    )
    pieces = line_reduce(keep, swap(send, "core"), z_lo)
    hidden = call(hidden_body, shape((rows // 8, hid), BF), *pieces)
    others = [lax.ppermute(hidden, "z_lo", [(i, i ^ step) for i in range(4)]) for step in (1, 2, 3)]
    half = call(join_body, shape((rows // 2, hid), BF), hidden, *others, scalars=(z_lo,))
    down = call(
        down_body, shape((rows, width), BF), half, swap(half, "core"), down_weight,
        scalars=(core,), flops=2 * rows * width * hid,
    )
    return lax.all_to_all(down.reshape(16, rows // 16, width), YX, split_axis=0, concat_axis=0, tiled=True)


def shards(
    tokens,
    queries,
    new_key,
    new_value,
    key_cache,
    value_cache,
    lengths,
    group_of,
    out_weight,
    norm_gain,
    gate_weight,
    up_weight,
    down_weight,
):
    groups = 32
    rows_dev, width = tokens.shape
    rows = group_of.shape[0]
    q_cols = queries.shape[1]
    cache_len = key_cache.shape[1]
    capacity = 2
    quarter = width // 4
    own_group = lax.axis_index(GRP)
    z_lo = lax.axis_index("z_lo")
    core = lax.axis_index("core")
    place_y = lax.axis_index("y")
    place_x = lax.axis_index("x")

    blocks = group_of.reshape(groups, rows_dev)
    mine = pick(blocks, own_group)
    earlier = jnp.arange(rows_dev)[:, None] > jnp.arange(rows_dev)[None, :]
    my_ranks = jnp.sum((mine[:, None] == mine[None, :]) & earlier, axis=1, dtype=jnp.int32)
    my_slots = mine * capacity + my_ranks
    selector = (jnp.arange(groups * capacity, dtype=jnp.int32)[:, None] == my_slots[None, :]).astype(BF)
    packed = jnp.concatenate([queries, new_key, new_value], axis=1)
    bucket = dot(selector, packed).astype(BF).reshape(groups, capacity, packed.shape[1])
    bucket, tokens_in = lax.optimization_barrier((bucket, tokens))
    received = lax.all_to_all(bucket, GRP, split_axis=0, concat_axis=0, tiled=True)

    flat_groups = group_of.reshape(rows)
    same = flat_groups[:, None] == flat_groups[None, :]
    index = jnp.arange(rows, dtype=jnp.int32)
    ahead = jnp.sum(same & (index[:, None] > index[None, :]), axis=1, dtype=jnp.int32)
    position = flat_groups * rows_dev + ahead
    halves = position.reshape(2, rows // 2, 1)
    in_block = index // rows_dev
    block_rank = jnp.sum(
        same & (index[:, None] > index[None, :]) & (in_block[:, None] == in_block[None, :]), axis=1, dtype=jnp.int32
    )
    slot_of = in_block * capacity + block_rank
    wanted = own_group * rows_dev + jnp.arange(rows_dev, dtype=jnp.int32)
    arrival = jnp.sum(
        jnp.where(position[None, :] == wanted[:, None], slot_of[None, :], 0), axis=1, keepdims=True, dtype=jnp.int32
    )

    tok = tokens_in.reshape(rows_dev, 4, quarter).transpose(1, 0, 2)
    tok = lax.all_to_all(tok, "x", split_axis=0, concat_axis=0, tiled=True)
    tok = lax.ppermute(tok.reshape(4 * rows_dev, quarter), AXES, [(b, a) for a, b in spread_pairs(0)])
    received, tok, arrival, halves = lax.optimization_barrier((received, tok, arrival, halves))

    heads = call(
        functools.partial(attend_body, rows_dev, cache_len, q_cols // HD),
        shape((rows_dev, q_cols), BF),
        arrival,
        received.reshape(groups * capacity, packed.shape[1]),
        key_cache.reshape(rows_dev * cache_len, HD),
        value_cache.reshape(rows_dev * cache_len, HD),
        lengths.reshape(rows_dev, 1),
    )
    heads = spread(heads, GRP, groups).reshape(rows, q_cols)
    outs = [shape((rows // 2, out_weight.shape[1]), BF)] * 2
    send, keep = call(
        project_body, outs, pick(halves, 1 - core), pick(halves, core), heads, out_weight,
        flops=4 * rows * q_cols * out_weight.shape[1],
    )
    own, one, two, three = line_reduce(keep, swap(send, "core"), z_lo)
    attn_out = (own + one.astype(F32) + two.astype(F32) + three.astype(F32)).astype(BF)
    residual = (tok.astype(F32) + attn_out.astype(F32)).astype(BF)
    near = lax.ppermute(residual, AXES, spread_pairs(0)).reshape(4, rows_dev, quarter)
    far = lax.ppermute(residual, AXES, spread_pairs(1)).reshape(4, rows_dev, quarter)

    gathered = spread(jnp.stack([near, far], axis=1).reshape(rows // 4, quarter), YX, 16)
    gathered = gathered.reshape(4, 4, rows // 4, quarter)
    parts = feed_forward(gathered, norm_gain.reshape(1, width), gate_weight, up_weight, down_weight, core, z_lo)
    sums = jnp.sum(parts.astype(F32), axis=0)
    ffn_out = sums[:rows_dev] + swap(sums[rows_dev:].astype(BF), "z_hi").astype(F32)
    kept = pick(gathered, place_y)
    kept = lax.dynamic_slice_in_dim(kept, place_x * 2 * rows_dev, rows_dev, axis=1)
    kept = kept.transpose(1, 0, 2).reshape(rows_dev, width)
    return (kept.astype(F32) + ffn_out).astype(BF)


def solution(mesh):
    fine = Mesh(np.asarray(mesh.devices).reshape(SIZES), AXES)
    in_specs = (
        P(GRP, TP),
        P(GRP, TP),
        P(GRP, TP),
        P(GRP, TP),
        P(GRP, None, TP),
        P(GRP, None, TP),
        P(GRP),
        P(),
        P(TP, GRP),
        P(TP),
        P(TP, GRP),
        P(TP, GRP),
        P(GRP, TP),
    )
    return jax.shard_map(shards, mesh=fine, in_specs=in_specs, out_specs=P(GRP, TP), check_vma=False)
```

```python
import functools
import math

import jax
import jax.numpy as jnp
import numpy as np
from jax import lax
from jax.experimental import pallas as pl
from jax.experimental.pallas import tpu as pltpu
from jax.sharding import Mesh
from jax.sharding import PartitionSpec as P

D = 16384
HD = 128
AXES = ("z_hi", "y", "x", "z_lo", "core")
SIZES = (2, 4, 4, 4, 2)
GRP = ("z_hi", "y", "x")
TP = ("z_lo", "core")
YX = ("y", "x")
BF = jnp.bfloat16
F32 = jnp.float32
MIB = 1 << 20
PAD = 896


def flat(z_hi, y, x, z_lo, core):
    return (((z_hi * 4 + y) * 4 + x) * 4 + z_lo) * 2 + core


def spread_pairs(flip):
    pairs = []
    for z_hi in range(2):
        for y in range(4):
            for x in range(4):
                for z_lo in range(4):
                    for core in range(2):
                        src = flat(z_hi, y, x, z_lo, core)
                        dst = flat(core ^ flip, z_lo, x, 2 * z_hi + y // 2, y % 2)
                        pairs.append((src, dst))
    return pairs


def swap(v, axis):
    return lax.ppermute(v, axis, [(0, 1), (1, 0)])


def pick(v, index):
    return lax.dynamic_index_in_dim(v, index, 0, keepdims=False)


def exchange(copies, *others):
    copies, *others = lax.optimization_barrier((copies, *others))
    got = lax.all_to_all(copies, YX, split_axis=0, concat_axis=0, tiled=True)
    return lax.optimization_barrier((got, *others))


def call(body, out_shape, *operands, scalars=(), streamed=(), scratch=(), limit=12):
    whole = pl.BlockSpec(memory_space=pltpu.VMEM)
    single = not isinstance(out_shape, (list, tuple))
    specs = [pl.BlockSpec(memory_space=pltpu.SMEM)] * len(scalars) + [whole] * len(operands)
    specs += [pl.BlockSpec(memory_space=pltpu.HBM)] * len(streamed)
    return pl.pallas_call(
        body,
        out_shape=out_shape,
        in_specs=specs,
        out_specs=whole if single else [whole] * len(out_shape),
        scratch_shapes=list(scratch),
        compiler_params=pltpu.CompilerParams(vmem_limit_bytes=limit * MIB),
        cost_estimate=pl.CostEstimate(flops=1, bytes_accessed=1, transcendentals=0),
    )(*[jnp.reshape(s, (1,)).astype(jnp.int32) for s in scalars], *operands, *streamed)


def shape(dims, dtype):
    return jax.ShapeDtypeStruct(dims, dtype)


def dot(a, b):
    return jnp.dot(a, b, preferred_element_type=F32)


def dot_t(a, b):
    return lax.dot_general(a, b, (((1,), (1,)), ((), ())), preferred_element_type=F32)


def attend_body(
    rows, cache_len, heads, place_x, slot_ref, got_ref, len_ref, own_tok, one_tok, two_tok, three_tok,
    key_ref, value_ref, out_ref,
):
    cols = own_tok.shape[1]
    for step, piece in enumerate((own_tok, one_tok, two_tok, three_tok)):
        group = place_x[0] ^ step
        at = pl.ds(pl.multiple_of(rows + (group & 1) * rows, rows), rows)
        out_ref[at, pl.ds(pl.multiple_of((group >> 1) * cols, cols), cols)] = piece[...]
    slots = lax.broadcasted_iota(jnp.int32, (rows, got_ref.shape[0]), 1)
    compact = (slot_ref[...] == slots).astype(F32).astype(BF)
    arrived = dot(compact, got_ref[...])
    q_cols = heads * HD
    rounded = arrived[:, :q_cols].astype(BF)
    tall = jnp.concatenate([rounded[:, j * HD : (j + 1) * HD] for j in range(heads)], axis=0)
    key_new = jnp.concatenate([arrived[:, q_cols : q_cols + HD]] * heads, axis=0)
    value_new = jnp.concatenate([arrived[:, q_cols + HD :]] * heads, axis=0)
    scale = 1.0 / math.sqrt(HD)
    own = jnp.sum(tall.astype(F32) * key_new, axis=1, keepdims=True) * scale
    scores = dot_t(tall, key_ref[...]) * scale
    spot = lax.broadcasted_iota(jnp.int32, scores.shape, 1)
    row = lax.rem(lax.broadcasted_iota(jnp.int32, scores.shape, 0), rows)
    start = row * cache_len
    lens = jnp.concatenate([len_ref[...]] * heads, axis=0)
    live = (spot >= start) & (spot < start + lens)
    masked = jnp.where(live, scores, -1e30)
    top = jnp.maximum(jnp.max(masked, axis=1, keepdims=True), own)
    exp_live = jnp.where(live, jnp.exp(masked - top), 0.0)
    exp_own = jnp.exp(own - top)
    total = jnp.sum(exp_live, axis=1, keepdims=True) + exp_own
    weights = (exp_live / total).astype(BF)
    own_weight = (exp_own / total).astype(BF).astype(F32)
    out = (dot(weights, value_ref[...]) + own_weight * value_new).astype(BF)
    for j in range(heads):
        out_ref[:rows, j * HD : (j + 1) * HD] = out[j * rows : (j + 1) * rows]


def project_body(send_pos, keep_pos, heads_ref, weight_ref, send_ref, keep_ref):
    product = dot(heads_ref[...], weight_ref[...]).astype(BF)
    for pos, out in ((send_pos, send_ref), (keep_pos, keep_ref)):
        spot = lax.broadcasted_iota(jnp.int32, (pos.shape[0], product.shape[0]), 1)
        unsort = (pos[...] == spot).astype(F32).astype(BF)
        out[...] = dot(unsort, product).astype(BF)


def split_body(z_lo, keep_ref, got_ref, own_ref, one_ref, two_ref, three_ref, mark_ref):
    rows = own_ref.shape[0]
    mark_ref[...] = jnp.zeros(mark_ref.shape, mark_ref.dtype)
    for step, out in enumerate((own_ref, one_ref, two_ref, three_ref)):
        at = pl.ds(pl.multiple_of((z_lo[0] ^ step) * rows, rows), rows)
        out[...] = (keep_ref[at, :].astype(F32) + got_ref[at, :].astype(F32)).astype(out.dtype)


MARK = jax.ShapeDtypeStruct((8, 128), F32)


def line_reduce(keep, got, z_lo):
    rows, cols = keep.shape[0] // 4, keep.shape[1]
    outs = [shape((rows, cols), F32)] + [shape((rows, cols), BF)] * 3 + [MARK]
    own, *pieces, mark = call(split_body, outs, keep, got, scalars=(z_lo,))
    return [own] + line_send(pieces), mark


def line_send(pieces):
    return [
        lax.ppermute(piece, "z_lo", [(i, i ^ step) for i in range(4)])
        for step, piece in zip((1, 2, 3), pieces)
    ]


def gate_up_body(core, rows_ref, gain_ref, gate_ref, up_ref, *refs):
    send_ref, keep_ref, mark_ref, total = refs[-4:]
    mark_ref[...] = jnp.zeros(mark_ref.shape, mark_ref.dtype)
    hid = gate_ref.shape[0]
    planes, blocks, count, cols = rows_ref.shape
    rows = planes * count
    squares = jnp.zeros((rows, 1), F32)
    parts = []
    for b in range(blocks):
        wide = rows_ref[:, b].reshape(rows, cols).astype(F32)
        squares += jnp.sum(wide * wide, axis=1, keepdims=True)
        parts.append((wide * gain_ref[:, b * cols : (b + 1) * cols].astype(F32)).astype(BF))
    scaled = jnp.concatenate(parts, axis=1)
    total[:, :hid] = dot_t(scaled, gate_ref[...])
    total[:, PAD : PAD + hid] = dot_t(scaled, up_ref[...])
    total[:, PAD + hid :] = jnp.zeros((rows, PAD - hid), F32)
    high = squares.astype(BF).astype(F32)
    lane = lax.broadcasted_iota(jnp.int32, (rows, PAD - hid), 1)
    total[:, hid:PAD] = jnp.where(lane == 0, high, jnp.where(lane == 1, squares - high, 0.0))
    half = rows // 2
    send_ref[...] = total[pl.ds(pl.multiple_of((1 - core[0]) * half, half), half), :].astype(BF)
    keep_ref[...] = total[pl.ds(pl.multiple_of(core[0] * half, half), half), :].astype(BF)


def hidden_body(own_ref, one_ref, two_ref, three_ref, mark_ref, out_ref):
    hid = out_ref.shape[1]
    sums = own_ref[...] + one_ref[...].astype(F32) + two_ref[...].astype(F32) + three_ref[...].astype(F32)
    mean_square = (sums[:, hid : hid + 1] + sums[:, hid + 1 : hid + 2]) / D
    inv = lax.rsqrt(mean_square + 1e-05)
    gate = sums[:, :hid] * inv
    up = sums[:, PAD : PAD + hid] * inv
    out_ref[...] = (gate / (1.0 + jnp.exp(-gate)) * up).astype(BF)


def join_body(z_lo, own_ref, one_ref, two_ref, three_ref, mark_ref, out_ref):
    rows = own_ref.shape[0]
    for step, piece in enumerate((own_ref, one_ref, two_ref, three_ref)):
        out_ref[pl.ds(pl.multiple_of((z_lo[0] ^ step) * rows, rows), rows), :] = piece[...]


def part_body(x, rows_ref, *outs):
    cols = outs[0].shape[1]
    for step, out in enumerate(outs):
        out[...] = rows_ref[:, pl.ds(pl.multiple_of((x[0] ^ step) * cols, cols), cols)]


def heads_body(rows, near_ref, far_ref, out_ref):
    for copy in range(out_ref.shape[0]):
        out_ref[copy, :rows] = near_ref[:rows]
        out_ref[copy, rows:] = far_ref[:rows]


def residual_body(rows, attn_ref, tok_ref, out_ref):
    cols = attn_ref.shape[1]
    for group in range(attn_ref.shape[0] // rows):
        at = rows + (group & 1) * rows
        side = (group >> 1) * cols
        tok = tok_ref[at : at + rows, side : side + cols].astype(F32)
        total = (attn_ref[group * rows : (group + 1) * rows].astype(F32) + tok).astype(BF)
        for copy in range(out_ref.shape[0]):
            out_ref[copy, group * rows : (group + 1) * rows] = total


def fold_body(parts_ref, out_ref):
    total = parts_ref[0].astype(F32)
    for part in range(1, parts_ref.shape[0]):
        total += parts_ref[part].astype(F32)
    out_ref[...] = total.astype(out_ref.dtype)


def down_body(core, own_ref, other_ref, weight_ref, out_ref, mark_ref):
    mark_ref[...] = jnp.zeros(mark_ref.shape, mark_ref.dtype)
    half = own_ref.shape[0]
    for place, rows_ref in ((core[0], own_ref), (1 - core[0], other_ref)):
        at = pl.ds(pl.multiple_of(place * half, half), half)
        out_ref[at, :] = dot(rows_ref[...], weight_ref[...]).astype(BF)


def gate_up(gathered, gain, gate_t, up_t, core, *marks):
    rows = gathered.shape[0] * gathered.shape[2]
    outs = [shape((rows // 2, 2 * PAD), BF)] * 2 + [MARK]
    return call(
        gate_up_body, outs, gathered, gain, gate_t, up_t, *marks,
        scalars=(core,), scratch=[pltpu.VMEM((rows, 2 * PAD), F32)], limit=20,
    )


def hidden_gather(pieces, hid, mark):
    hidden = call(hidden_body, shape((pieces[0].shape[0], hid), BF), *pieces, mark)
    return [hidden] + line_send([hidden] * 3)


def down_project(pieces, down_weight, z_lo, core, mark):
    quarter, hid = pieces[0].shape
    width = down_weight.shape[1]
    half = call(join_body, shape((4 * quarter, hid), BF), *pieces, mark, scalars=(z_lo,))
    return call(
        down_body, [shape((8 * quarter, width), BF), MARK], half, swap(half, "core"), down_weight,
        scalars=(core,), limit=16,
    )


def all_to_all(v, axes):
    return lax.all_to_all(v, axes, split_axis=0, concat_axis=0, tiled=True)


def shards(
    tokens,
    queries,
    new_key,
    new_value,
    key_cache,
    value_cache,
    lengths,
    group_of,
    out_weight,
    norm_gain,
    gate_weight,
    up_weight,
    down_weight,
):
    groups = 32
    rows_dev, width = tokens.shape
    rows = group_of.shape[0]
    q_cols = queries.shape[1]
    cache_len = key_cache.shape[1]
    capacity = 2
    quarter = width // 4
    own_group = lax.axis_index(GRP)
    z_lo = lax.axis_index("z_lo")
    core = lax.axis_index("core")
    place_z = lax.axis_index("z_hi")
    place_y = lax.axis_index("y")
    place_x = lax.axis_index("x")

    blocks = group_of.reshape(groups, rows_dev)
    mine = pick(blocks, own_group)
    earlier = jnp.arange(rows_dev)[:, None] > jnp.arange(rows_dev)[None, :]
    my_ranks = jnp.sum((mine[:, None] == mine[None, :]) & earlier, axis=1, dtype=jnp.int32)
    my_slots = mine * capacity + my_ranks
    selector = (jnp.arange(groups * capacity, dtype=jnp.int32)[:, None] == my_slots[None, :]).astype(BF)
    packed = jnp.concatenate([queries, new_key, new_value], axis=1)
    bucket = dot(selector, packed).astype(BF).reshape(groups, capacity, packed.shape[1])
    bucket, tokens_in = lax.optimization_barrier((bucket, tokens))
    received = lax.all_to_all(bucket, GRP, split_axis=0, concat_axis=0, tiled=True)

    flat_groups = group_of.reshape(rows)
    same = flat_groups[:, None] == flat_groups[None, :]
    index = jnp.arange(rows, dtype=jnp.int32)
    before = same & (index[:, None] > index[None, :])
    in_block = index // rows_dev
    ahead = jnp.sum(before, axis=1, dtype=jnp.int32)
    block_rank = jnp.sum(before & (in_block[:, None] == in_block[None, :]), axis=1, dtype=jnp.int32)
    slot_of = in_block * capacity + block_rank
    wanted = own_group * rows_dev + jnp.arange(rows_dev, dtype=jnp.int32)
    position = flat_groups * rows_dev + ahead
    arrival = jnp.sum(
        jnp.where(position[None, :] == wanted[:, None], slot_of[None, :], 0), axis=1, keepdims=True, dtype=jnp.int32
    )
    plane = groups // 2
    gathered_at = ((flat_groups % plane) * 2 + (flat_groups // plane ^ place_z)) * rows_dev + ahead
    halves = gathered_at.reshape(2, rows // 2, 1)
    send_pos, keep_pos = pick(halves, 1 - core), pick(halves, core)

    pieces = call(part_body, [shape((rows_dev, quarter), BF)] * 4, tokens_in, scalars=(place_x,))
    pieces = [pieces[0]] + [
        lax.ppermute(pieces[step], "x", [(i, i ^ step) for i in range(4)]) for step in (1, 2, 3)
    ]

    caches = [cache.reshape(rows_dev * cache_len, HD) for cache in (key_cache, value_cache)]
    heads = call(
        functools.partial(attend_body, rows_dev, cache_len, q_cols // HD),
        shape((3 * rows_dev, q_cols), BF),
        arrival,
        received.reshape(groups * capacity, packed.shape[1]),
        lengths.reshape(rows_dev, 1),
        *pieces,
        *caches,
        scalars=(place_x,),
    )
    far_heads = swap(heads, "z_hi")
    copies = call(
        functools.partial(heads_body, rows_dev), shape((plane, 2 * rows_dev, q_cols), BF), heads, far_heads
    )
    gathered, send_pos, keep_pos = exchange(copies, send_pos, keep_pos)
    outs = [shape((rows // 2, out_weight.shape[1]), BF)] * 2
    send, keep = call(
        project_body, outs, send_pos, keep_pos, gathered.reshape(rows, q_cols), out_weight,
    )
    (own, one, two, three), _ = line_reduce(keep, swap(send, "core"), z_lo)
    attn_out = (own + one.astype(F32) + two.astype(F32) + three.astype(F32)).astype(BF)
    far = lax.ppermute(attn_out, AXES, spread_pairs(1))
    near = lax.ppermute(attn_out, AXES, spread_pairs(0))
    gain = norm_gain.reshape(1, width)
    hid = down_weight.shape[0]
    gate_t, up_t = gate_weight.T, up_weight.T
    gathered = []
    for attn, tok in ((far, far_heads), (near, heads)):
        copies = call(
            functools.partial(residual_body, rows_dev), shape((plane, rows // 8, quarter), BF), attn, tok
        )
        gathered.append(all_to_all(copies, YX).reshape(4, 4, rows // 8, quarter))
    far_send, far_keep, _ = gate_up(gathered[0], gain, gate_t, up_t, core)
    far_pieces, far_sent = line_reduce(far_keep, swap(far_send, "core"), z_lo)
    near_gathered = gathered[1]
    near_send, near_keep, near_done = gate_up(near_gathered, gain, gate_t, up_t, core, far_sent)
    far_hidden = call(hidden_body, shape((far_pieces[0].shape[0], hid), BF), *far_pieces, near_done)
    near_send, far_hidden = lax.optimization_barrier((near_send, far_hidden))
    near_pieces, near_sent = line_reduce(near_keep, swap(near_send, "core"), z_lo)
    far_hidden = [far_hidden] + line_send([far_hidden] * 3)
    far_down, far_done = down_project(far_hidden, down_weight, z_lo, core, near_sent)
    far_down, near_pieces = lax.optimization_barrier((far_down, near_pieces))
    far_parts = all_to_all(far_down.reshape(plane, rows_dev, width), YX)
    near_hidden = hidden_gather(near_pieces, hid, far_done)
    near_down, near_done = down_project(near_hidden, down_weight, z_lo, core, far_done)
    near_parts = all_to_all(near_down.reshape(plane, rows_dev, width), YX)
    kept = lax.dynamic_slice_in_dim(pick(near_gathered, place_y), place_x * rows_dev, rows_dev, axis=1)
    kept = kept.transpose(1, 0, 2).reshape(rows_dev, width)
    far_sum = call(fold_body, shape((rows_dev, width), BF), far_parts)
    near_sum = call(fold_body, shape((rows_dev, width), F32), near_parts)
    return (kept.astype(F32) + (near_sum + swap(far_sum, "z_hi").astype(F32))).astype(BF)


def solution(mesh):
    fine = Mesh(np.asarray(mesh.devices).reshape(SIZES), AXES)
    in_specs = (
        P(GRP, TP),
        P(GRP, TP),
        P(GRP, TP),
        P(GRP, TP),
        P(GRP, None, TP),
        P(GRP, None, TP),
        P(GRP),
        P(),
        P(TP, GRP),
        P(TP),
        P(TP, GRP),
        P(TP, GRP),
        P(GRP, TP),
    )
    return jax.shard_map(shards, mesh=fine, in_specs=in_specs, out_specs=P(GRP, TP), check_vma=False)
```

```python
import functools
import math

import jax
import jax.numpy as jnp
import numpy as np
from jax import lax
from jax.experimental import pallas as pl
from jax.experimental.pallas import tpu as pltpu
from jax.sharding import Mesh
from jax.sharding import PartitionSpec as P

D = 16384
HD = 128
AXES = ("z_hi", "y", "x", "z_lo", "core")
SIZES = (2, 4, 4, 4, 2)
GRP = ("z_hi", "y", "x")
TP = ("z_lo", "core")
YX = ("y", "x")
BF = jnp.bfloat16
F32 = jnp.float32
MIB = 1 << 20
LONG = 30_000_000_000
PAD = 896


def flat(z_hi, y, x, z_lo, core):
    return (((z_hi * 4 + y) * 4 + x) * 4 + z_lo) * 2 + core


def spread_pairs(flip):
    pairs = []
    for z_hi in range(2):
        for y in range(4):
            for x in range(4):
                for z_lo in range(4):
                    for core in range(2):
                        src = flat(z_hi, y, x, z_lo, core)
                        dst = flat(core ^ flip, z_lo, x, 2 * z_hi + y // 2, y % 2)
                        pairs.append((src, dst))
    return pairs


def swap(v, axis):
    return lax.ppermute(v, axis, [(0, 1), (1, 0)])


def pick(v, index):
    return lax.dynamic_index_in_dim(v, index, 0, keepdims=False)


def exchange(copies, *others):
    copies, *others = lax.optimization_barrier((copies, *others))
    got = lax.all_to_all(copies, YX, split_axis=0, concat_axis=0, tiled=True)
    return lax.optimization_barrier((got, *others))


def call(body, out_shape, *operands, scalars=(), streamed=(), scratch=(), limit=12, weight=1):
    whole = pl.BlockSpec(memory_space=pltpu.VMEM)
    single = not isinstance(out_shape, (list, tuple))
    specs = [pl.BlockSpec(memory_space=pltpu.SMEM)] * len(scalars) + [whole] * len(operands)
    specs += [pl.BlockSpec(memory_space=pltpu.HBM)] * len(streamed)
    return pl.pallas_call(
        body,
        out_shape=out_shape,
        in_specs=specs,
        out_specs=whole if single else [whole] * len(out_shape),
        scratch_shapes=list(scratch),
        compiler_params=pltpu.CompilerParams(vmem_limit_bytes=limit * MIB),
        cost_estimate=pl.CostEstimate(flops=weight, bytes_accessed=1, transcendentals=0),
    )(*[jnp.reshape(s, (1,)).astype(jnp.int32) for s in scalars], *operands, *streamed)


def shape(dims, dtype):
    return jax.ShapeDtypeStruct(dims, dtype)


def dot(a, b):
    return jnp.dot(a, b, preferred_element_type=F32)


def dot_t(a, b):
    return lax.dot_general(a, b, (((1,), (1,)), ((), ())), preferred_element_type=F32)


def attend_body(
    rows, cache_len, heads, place_x, slot_ref, got_ref, len_ref, own_tok, one_tok, two_tok, three_tok,
    key_ref, value_ref, out_ref,
):
    cols = own_tok.shape[1]
    for step, piece in enumerate((own_tok, one_tok, two_tok, three_tok)):
        group = place_x[0] ^ step
        at = pl.ds(pl.multiple_of(rows + (group & 1) * rows, rows), rows)
        out_ref[at, pl.ds(pl.multiple_of((group >> 1) * cols, cols), cols)] = piece[...]
    slots = lax.broadcasted_iota(jnp.int32, (rows, got_ref.shape[0]), 1)
    compact = (slot_ref[...] == slots).astype(F32).astype(BF)
    arrived = dot(compact, got_ref[...])
    q_cols = heads * HD
    rounded = arrived[:, :q_cols].astype(BF)
    tall = jnp.concatenate([rounded[:, j * HD : (j + 1) * HD] for j in range(heads)], axis=0)
    key_new = jnp.concatenate([arrived[:, q_cols : q_cols + HD]] * heads, axis=0)
    value_new = jnp.concatenate([arrived[:, q_cols + HD :]] * heads, axis=0)
    scale = 1.0 / math.sqrt(HD)
    own = jnp.sum(tall.astype(F32) * key_new, axis=1, keepdims=True) * scale
    scores = dot_t(tall, key_ref[...]) * scale
    spot = lax.broadcasted_iota(jnp.int32, scores.shape, 1)
    row = lax.rem(lax.broadcasted_iota(jnp.int32, scores.shape, 0), rows)
    start = row * cache_len
    lens = jnp.concatenate([len_ref[...]] * heads, axis=0)
    live = (spot >= start) & (spot < start + lens)
    masked = jnp.where(live, scores, -1e30)
    top = jnp.maximum(jnp.max(masked, axis=1, keepdims=True), own)
    exp_live = jnp.where(live, jnp.exp(masked - top), 0.0)
    exp_own = jnp.exp(own - top)
    total = jnp.sum(exp_live, axis=1, keepdims=True) + exp_own
    weights = (exp_live / total).astype(BF)
    own_weight = (exp_own / total).astype(BF).astype(F32)
    out = (dot(weights, value_ref[...]) + own_weight * value_new).astype(BF)
    for j in range(heads):
        out_ref[:rows, j * HD : (j + 1) * HD] = out[j * rows : (j + 1) * rows]


def project_body(send_pos, keep_pos, heads_ref, weight_ref, send_ref, keep_ref):
    product = dot(heads_ref[...], weight_ref[...]).astype(BF)
    for pos, out in ((send_pos, send_ref), (keep_pos, keep_ref)):
        spot = lax.broadcasted_iota(jnp.int32, (pos.shape[0], product.shape[0]), 1)
        unsort = (pos[...] == spot).astype(F32).astype(BF)
        out[...] = dot(unsort, product).astype(BF)


def split_body(z_lo, keep_ref, got_ref, own_ref, one_ref, two_ref, three_ref, mark_ref):
    rows = own_ref.shape[0]
    mark_ref[...] = jnp.zeros(mark_ref.shape, mark_ref.dtype)
    for step, out in enumerate((own_ref, one_ref, two_ref, three_ref)):
        at = pl.ds(pl.multiple_of((z_lo[0] ^ step) * rows, rows), rows)
        out[...] = (keep_ref[at, :].astype(F32) + got_ref[at, :].astype(F32)).astype(out.dtype)


MARK = jax.ShapeDtypeStruct((8, 128), F32)


def line_reduce(keep, got, z_lo):
    rows, cols = keep.shape[0] // 4, keep.shape[1]
    outs = [shape((rows, cols), F32)] + [shape((rows, cols), BF)] * 3 + [MARK]
    own, *pieces, mark = call(split_body, outs, keep, got, scalars=(z_lo,))
    return [own] + line_send(pieces), mark


def line_send(pieces):
    return [
        lax.ppermute(piece, "z_lo", [(i, i ^ step) for i in range(4)])
        for step, piece in zip((1, 2, 3), pieces)
    ]


def gate_up_body(core, rows_ref, gain_ref, gate_ref, up_ref, *refs):
    send_ref, keep_ref, mark_ref, total = refs[-4:]
    mark_ref[...] = jnp.zeros(mark_ref.shape, mark_ref.dtype)
    hid = gate_ref.shape[0]
    planes, blocks, count, cols = rows_ref.shape
    rows = planes * count
    squares = jnp.zeros((rows, 1), F32)
    parts = []
    for b in range(blocks):
        wide = rows_ref[:, b].reshape(rows, cols).astype(F32)
        squares += jnp.sum(wide * wide, axis=1, keepdims=True)
        parts.append((wide * gain_ref[:, b * cols : (b + 1) * cols].astype(F32)).astype(BF))
    scaled = jnp.concatenate(parts, axis=1)
    total[:, :hid] = dot_t(scaled, gate_ref[...])
    total[:, PAD : PAD + hid] = dot_t(scaled, up_ref[...])
    total[:, PAD + hid :] = jnp.zeros((rows, PAD - hid), F32)
    high = squares.astype(BF).astype(F32)
    lane = lax.broadcasted_iota(jnp.int32, (rows, PAD - hid), 1)
    total[:, hid:PAD] = jnp.where(lane == 0, high, jnp.where(lane == 1, squares - high, 0.0))
    half = rows // 2
    send_ref[...] = total[pl.ds(pl.multiple_of((1 - core[0]) * half, half), half), :].astype(BF)
    keep_ref[...] = total[pl.ds(pl.multiple_of(core[0] * half, half), half), :].astype(BF)


def hidden_body(own_ref, one_ref, two_ref, three_ref, mark_ref, out_ref):
    hid = out_ref.shape[1]
    sums = own_ref[...] + one_ref[...].astype(F32) + two_ref[...].astype(F32) + three_ref[...].astype(F32)
    mean_square = (sums[:, hid : hid + 1] + sums[:, hid + 1 : hid + 2]) / D
    inv = lax.rsqrt(mean_square + 1e-05)
    gate = sums[:, :hid] * inv
    up = sums[:, PAD : PAD + hid] * inv
    out_ref[...] = (gate / (1.0 + jnp.exp(-gate)) * up).astype(BF)


def join_body(z_lo, own_ref, one_ref, two_ref, three_ref, mark_ref, out_ref):
    rows = own_ref.shape[0]
    for step, piece in enumerate((own_ref, one_ref, two_ref, three_ref)):
        out_ref[pl.ds(pl.multiple_of((z_lo[0] ^ step) * rows, rows), rows), :] = piece[...]


def part_body(x, rows_ref, *outs):
    cols = outs[0].shape[1]
    for step, out in enumerate(outs):
        out[...] = rows_ref[:, pl.ds(pl.multiple_of((x[0] ^ step) * cols, cols), cols)]


def heads_body(rows, near_ref, far_ref, out_ref):
    for copy in range(out_ref.shape[0]):
        out_ref[copy, :rows] = near_ref[:rows]
        out_ref[copy, rows:] = far_ref[:rows]


def residual_body(rows, attn_ref, tok_ref, out_ref):
    cols = attn_ref.shape[1]
    for group in range(attn_ref.shape[0] // rows):
        at = rows + (group & 1) * rows
        side = (group >> 1) * cols
        tok = tok_ref[at : at + rows, side : side + cols].astype(F32)
        total = (attn_ref[group * rows : (group + 1) * rows].astype(F32) + tok).astype(BF)
        for copy in range(out_ref.shape[0]):
            out_ref[copy, group * rows : (group + 1) * rows] = total


def fold_body(parts_ref, out_ref):
    total = parts_ref[0].astype(F32)
    for part in range(1, parts_ref.shape[0]):
        total += parts_ref[part].astype(F32)
    out_ref[...] = total.astype(out_ref.dtype)


def down_body(core, own_ref, other_ref, weight_ref, out_ref, mark_ref):
    mark_ref[...] = jnp.zeros(mark_ref.shape, mark_ref.dtype)
    half = own_ref.shape[0]
    for place, rows_ref in ((core[0], own_ref), (1 - core[0], other_ref)):
        at = pl.ds(pl.multiple_of(place * half, half), half)
        out_ref[at, :] = dot(rows_ref[...], weight_ref[...]).astype(BF)


def gate_up(gathered, gain, gate_t, up_t, core, *marks):
    rows = gathered.shape[0] * gathered.shape[2]
    outs = [shape((rows // 2, 2 * PAD), BF)] * 2 + [MARK]
    return call(
        gate_up_body, outs, gathered, gain, gate_t, up_t, *marks,
        scalars=(core,), scratch=[pltpu.VMEM((rows, 2 * PAD), F32)], limit=20,
    )


def hidden_gather(pieces, hid, mark):
    hidden = call(hidden_body, shape((pieces[0].shape[0], hid), BF), *pieces, mark, weight=LONG)
    return [hidden] + line_send([hidden] * 3)


def down_project(pieces, down_weight, z_lo, core, mark):
    quarter, hid = pieces[0].shape
    width = down_weight.shape[1]
    half = call(join_body, shape((4 * quarter, hid), BF), *pieces, mark, scalars=(z_lo,))
    return call(
        down_body, [shape((8 * quarter, width), BF), MARK], half, swap(half, "core"), down_weight,
        scalars=(core,), limit=16,
    )


def all_to_all(v, axes):
    return lax.all_to_all(v, axes, split_axis=0, concat_axis=0, tiled=True)


def shards(
    tokens,
    queries,
    new_key,
    new_value,
    key_cache,
    value_cache,
    lengths,
    group_of,
    out_weight,
    norm_gain,
    gate_weight,
    up_weight,
    down_weight,
):
    groups = 32
    rows_dev, width = tokens.shape
    rows = group_of.shape[0]
    q_cols = queries.shape[1]
    cache_len = key_cache.shape[1]
    capacity = 2
    quarter = width // 4
    own_group = lax.axis_index(GRP)
    z_lo = lax.axis_index("z_lo")
    core = lax.axis_index("core")
    place_z = lax.axis_index("z_hi")
    place_y = lax.axis_index("y")
    place_x = lax.axis_index("x")

    blocks = group_of.reshape(groups, rows_dev)
    mine = pick(blocks, own_group)
    earlier = jnp.arange(rows_dev)[:, None] > jnp.arange(rows_dev)[None, :]
    my_ranks = jnp.sum((mine[:, None] == mine[None, :]) & earlier, axis=1, dtype=jnp.int32)
    my_slots = mine * capacity + my_ranks
    selector = (jnp.arange(groups * capacity, dtype=jnp.int32)[:, None] == my_slots[None, :]).astype(BF)
    packed = jnp.concatenate([queries, new_key, new_value], axis=1)
    bucket = dot(selector, packed).astype(BF).reshape(groups, capacity, packed.shape[1])
    bucket, tokens_in = lax.optimization_barrier((bucket, tokens))
    received = lax.all_to_all(bucket, GRP, split_axis=0, concat_axis=0, tiled=True)

    flat_groups = group_of.reshape(rows)
    same = flat_groups[:, None] == flat_groups[None, :]
    index = jnp.arange(rows, dtype=jnp.int32)
    before = same & (index[:, None] > index[None, :])
    in_block = index // rows_dev
    ahead = jnp.sum(before, axis=1, dtype=jnp.int32)
    block_rank = jnp.sum(before & (in_block[:, None] == in_block[None, :]), axis=1, dtype=jnp.int32)
    slot_of = in_block * capacity + block_rank
    wanted = own_group * rows_dev + jnp.arange(rows_dev, dtype=jnp.int32)
    position = flat_groups * rows_dev + ahead
    arrival = jnp.sum(
        jnp.where(position[None, :] == wanted[:, None], slot_of[None, :], 0), axis=1, keepdims=True, dtype=jnp.int32
    )
    plane = groups // 2
    gathered_at = ((flat_groups % plane) * 2 + (flat_groups // plane ^ place_z)) * rows_dev + ahead
    halves = gathered_at.reshape(2, rows // 2, 1)
    send_pos, keep_pos = pick(halves, 1 - core), pick(halves, core)

    pieces = call(part_body, [shape((rows_dev, quarter), BF)] * 4, tokens_in, scalars=(place_x,))
    pieces = [pieces[0]] + [
        lax.ppermute(pieces[step], "x", [(i, i ^ step) for i in range(4)]) for step in (1, 2, 3)
    ]

    caches = [cache.reshape(rows_dev * cache_len, HD) for cache in (key_cache, value_cache)]
    heads = call(
        functools.partial(attend_body, rows_dev, cache_len, q_cols // HD),
        shape((3 * rows_dev, q_cols), BF),
        arrival,
        received.reshape(groups * capacity, packed.shape[1]),
        lengths.reshape(rows_dev, 1),
        *pieces,
        *caches,
        scalars=(place_x,),
    )
    far_heads = swap(heads, "z_hi")
    copies = call(
        functools.partial(heads_body, rows_dev), shape((plane, 2 * rows_dev, q_cols), BF), heads, far_heads
    )
    gathered, send_pos, keep_pos = exchange(copies, send_pos, keep_pos)
    outs = [shape((rows // 2, out_weight.shape[1]), BF)] * 2
    send, keep = call(
        project_body, outs, send_pos, keep_pos, gathered.reshape(rows, q_cols), out_weight,
    )
    (own, one, two, three), _ = line_reduce(keep, swap(send, "core"), z_lo)
    attn_out = (own + one.astype(F32) + two.astype(F32) + three.astype(F32)).astype(BF)
    far = lax.ppermute(attn_out, AXES, spread_pairs(1))
    near = lax.ppermute(attn_out, AXES, spread_pairs(0))
    gain = norm_gain.reshape(1, width)
    hid = down_weight.shape[0]
    gate_t, up_t = gate_weight.T, up_weight.T
    gathered = []
    for attn, tok in ((far, far_heads), (near, heads)):
        copies = call(
            functools.partial(residual_body, rows_dev), shape((plane, rows // 8, quarter), BF), attn, tok
        )
        gathered.append(all_to_all(copies, YX).reshape(4, 4, rows // 8, quarter))
    far_send, far_keep, _ = gate_up(gathered[0], gain, gate_t, up_t, core)
    far_pieces, far_sent = line_reduce(far_keep, swap(far_send, "core"), z_lo)
    near_gathered = gathered[1]
    near_send, near_keep, near_done = gate_up(near_gathered, gain, gate_t, up_t, core, far_sent)
    far_hidden = call(hidden_body, shape((far_pieces[0].shape[0], hid), BF), *far_pieces, near_done)
    near_send, far_hidden = lax.optimization_barrier((near_send, far_hidden))
    near_pieces, near_sent = line_reduce(near_keep, swap(near_send, "core"), z_lo)
    far_hidden = [far_hidden] + line_send([far_hidden] * 3)
    far_down, far_done = down_project(far_hidden, down_weight, z_lo, core, near_sent)
    far_parts = all_to_all(far_down.reshape(plane, rows_dev, width), YX)
    near_hidden = hidden_gather(near_pieces, hid, far_done)
    near_down, near_done = down_project(near_hidden, down_weight, z_lo, core, far_done)
    near_parts = all_to_all(near_down.reshape(plane, rows_dev, width), YX)
    kept = lax.dynamic_slice_in_dim(pick(near_gathered, place_y), place_x * rows_dev, rows_dev, axis=1)
    kept = kept.transpose(1, 0, 2).reshape(rows_dev, width)
    far_sum = call(fold_body, shape((rows_dev, width), BF), far_parts)
    near_sum = call(fold_body, shape((rows_dev, width), F32), near_parts)
    return (kept.astype(F32) + (near_sum + swap(far_sum, "z_hi").astype(F32))).astype(BF)


def solution(mesh):
    fine = Mesh(np.asarray(mesh.devices).reshape(SIZES), AXES)
    in_specs = (
        P(GRP, TP),
        P(GRP, TP),
        P(GRP, TP),
        P(GRP, TP),
        P(GRP, None, TP),
        P(GRP, None, TP),
        P(GRP),
        P(),
        P(TP, GRP),
        P(TP),
        P(TP, GRP),
        P(TP, GRP),
        P(GRP, TP),
    )
    return jax.shard_map(shards, mesh=fine, in_specs=in_specs, out_specs=P(GRP, TP), check_vma=False)
```

```python
import functools
import math

import jax
import jax.numpy as jnp
import numpy as np
from jax import lax
from jax.experimental import pallas as pl
from jax.experimental.pallas import tpu as pltpu
from jax.sharding import Mesh
from jax.sharding import PartitionSpec as P

D = 16384
HD = 128
AXES = ("z_hi", "y", "x", "z_lo", "core")
SIZES = (2, 4, 4, 4, 2)
GRP = ("z_hi", "y", "x")
TP = ("z_lo", "core")
YX = ("y", "x")
BF = jnp.bfloat16
F32 = jnp.float32
MIB = 1 << 20
LONG = 30_000_000_000
PAD = 896


def flat(z_hi, y, x, z_lo, core):
    return (((z_hi * 4 + y) * 4 + x) * 4 + z_lo) * 2 + core


def spread_pairs(flip):
    pairs = []
    for z_hi in range(2):
        for y in range(4):
            for x in range(4):
                for z_lo in range(4):
                    for core in range(2):
                        src = flat(z_hi, y, x, z_lo, core)
                        dst = flat(core ^ flip, z_lo, x, 2 * z_hi + y // 2, y % 2)
                        pairs.append((src, dst))
    return pairs


def swap(v, axis):
    return lax.ppermute(v, axis, [(0, 1), (1, 0)])


def pick(v, index):
    return lax.dynamic_index_in_dim(v, index, 0, keepdims=False)


def exchange(copies, *others):
    copies, *others = lax.optimization_barrier((copies, *others))
    got = lax.all_to_all(copies, YX, split_axis=0, concat_axis=0, tiled=True)
    return lax.optimization_barrier((got, *others))


def call(body, out_shape, *operands, scalars=(), streamed=(), scratch=(), limit=12, weight=1):
    whole = pl.BlockSpec(memory_space=pltpu.VMEM)
    single = not isinstance(out_shape, (list, tuple))
    specs = [pl.BlockSpec(memory_space=pltpu.SMEM)] * len(scalars) + [whole] * len(operands)
    specs += [pl.BlockSpec(memory_space=pltpu.HBM)] * len(streamed)
    return pl.pallas_call(
        body,
        out_shape=out_shape,
        in_specs=specs,
        out_specs=whole if single else [whole] * len(out_shape),
        scratch_shapes=list(scratch),
        compiler_params=pltpu.CompilerParams(vmem_limit_bytes=limit * MIB),
        cost_estimate=pl.CostEstimate(flops=weight, bytes_accessed=1, transcendentals=0),
    )(*[jnp.reshape(s, (1,)).astype(jnp.int32) for s in scalars], *operands, *streamed)


def shape(dims, dtype):
    return jax.ShapeDtypeStruct(dims, dtype)


def dot(a, b):
    return jnp.dot(a, b, preferred_element_type=F32)


def dot_t(a, b):
    return lax.dot_general(a, b, (((1,), (1,)), ((), ())), preferred_element_type=F32)


def attend_body(
    rows, cache_len, heads, place_x, slot_ref, got_ref, len_ref, own_tok, one_tok, two_tok, three_tok,
    key_ref, value_ref, out_ref,
):
    cols = own_tok.shape[1]
    for step, piece in enumerate((own_tok, one_tok, two_tok, three_tok)):
        group = place_x[0] ^ step
        at = pl.ds(pl.multiple_of(rows + (group & 1) * rows, rows), rows)
        out_ref[at, pl.ds(pl.multiple_of((group >> 1) * cols, cols), cols)] = piece[...]
    slots = lax.broadcasted_iota(jnp.int32, (rows, got_ref.shape[0]), 1)
    compact = (slot_ref[...] == slots).astype(F32).astype(BF)
    arrived = dot(compact, got_ref[...])
    q_cols = heads * HD
    rounded = arrived[:, :q_cols].astype(BF)
    tall = jnp.concatenate([rounded[:, j * HD : (j + 1) * HD] for j in range(heads)], axis=0)
    key_new = jnp.concatenate([arrived[:, q_cols : q_cols + HD]] * heads, axis=0)
    value_new = jnp.concatenate([arrived[:, q_cols + HD :]] * heads, axis=0)
    scale = 1.0 / math.sqrt(HD)
    own = jnp.sum(tall.astype(F32) * key_new, axis=1, keepdims=True) * scale
    scores = dot_t(tall, key_ref[...]) * scale
    spot = lax.broadcasted_iota(jnp.int32, scores.shape, 1)
    row = lax.rem(lax.broadcasted_iota(jnp.int32, scores.shape, 0), rows)
    start = row * cache_len
    lens = jnp.concatenate([len_ref[...]] * heads, axis=0)
    live = (spot >= start) & (spot < start + lens)
    masked = jnp.where(live, scores, -1e30)
    top = jnp.maximum(jnp.max(masked, axis=1, keepdims=True), own)
    exp_live = jnp.where(live, jnp.exp(masked - top), 0.0)
    exp_own = jnp.exp(own - top)
    total = jnp.sum(exp_live, axis=1, keepdims=True) + exp_own
    weights = (exp_live / total).astype(BF)
    own_weight = (exp_own / total).astype(BF).astype(F32)
    out = (dot(weights, value_ref[...]) + own_weight * value_new).astype(BF)
    for j in range(heads):
        out_ref[:rows, j * HD : (j + 1) * HD] = out[j * rows : (j + 1) * rows]


def project_body(send_pos, keep_pos, heads_ref, weight_ref, send_ref, keep_ref):
    product = dot(heads_ref[...], weight_ref[...]).astype(BF)
    for pos, out in ((send_pos, send_ref), (keep_pos, keep_ref)):
        spot = lax.broadcasted_iota(jnp.int32, (pos.shape[0], product.shape[0]), 1)
        unsort = (pos[...] == spot).astype(F32).astype(BF)
        out[...] = dot(unsort, product).astype(BF)


def split_body(z_lo, keep_ref, got_ref, own_ref, one_ref, two_ref, three_ref, mark_ref):
    rows = own_ref.shape[0]
    mark_ref[...] = jnp.zeros(mark_ref.shape, mark_ref.dtype)
    for step, out in enumerate((own_ref, one_ref, two_ref, three_ref)):
        at = pl.ds(pl.multiple_of((z_lo[0] ^ step) * rows, rows), rows)
        out[...] = (keep_ref[at, :].astype(F32) + got_ref[at, :].astype(F32)).astype(out.dtype)


MARK = jax.ShapeDtypeStruct((8, 128), F32)


def line_reduce(keep, got, z_lo):
    rows, cols = keep.shape[0] // 4, keep.shape[1]
    outs = [shape((rows, cols), BF)] * 4 + [MARK]
    own, *pieces, mark = call(split_body, outs, keep, got, scalars=(z_lo,))
    return [own] + line_send(pieces), mark


def line_send(pieces):
    return [
        lax.ppermute(piece, "z_lo", [(i, i ^ step) for i in range(4)])
        for step, piece in zip((1, 2, 3), pieces)
    ]


def gate_body(rows_ref, gain_ref, gate_ref, *refs):
    scaled_ref, part_ref = refs[-2:]
    hid = gate_ref.shape[0]
    planes, blocks, count, cols = rows_ref.shape
    rows = planes * count
    squares = jnp.zeros((rows, 1), F32)
    for b in range(blocks):
        wide = rows_ref[:, b].reshape(rows, cols).astype(F32)
        squares += jnp.sum(wide * wide, axis=1, keepdims=True)
        at = slice(b * cols, (b + 1) * cols)
        scaled_ref[:, at] = (wide * gain_ref[:, at].astype(F32)).astype(BF)
    part_ref[:, :hid] = dot_t(scaled_ref[...], gate_ref[...]).astype(BF)
    high = squares.astype(BF).astype(F32)
    lane = lax.broadcasted_iota(jnp.int32, (rows, PAD - hid), 1)
    part_ref[:, hid:] = jnp.where(lane == 0, high, jnp.where(lane == 1, squares - high, 0.0)).astype(BF)


def up_body(core, scaled_ref, part_ref, up_ref, send_ref, keep_ref, mark_ref, total):
    mark_ref[...] = jnp.zeros(mark_ref.shape, mark_ref.dtype)
    rows, hid = scaled_ref.shape[0], up_ref.shape[0]
    half = rows // 2
    total[:, :hid] = dot_t(scaled_ref[...], up_ref[...])
    total[:, hid:] = jnp.zeros((rows, PAD - hid), F32)
    for place, out in ((1 - core[0], send_ref), (core[0], keep_ref)):
        at = pl.ds(pl.multiple_of(place * half, half), half)
        out[:, :PAD] = part_ref[at, :]
        out[:, PAD:] = total[at, :].astype(BF)


def hidden_body(own_ref, one_ref, two_ref, three_ref, mark_ref, out_ref):
    hid = out_ref.shape[1]
    sums = own_ref[...].astype(F32) + one_ref[...].astype(F32) + two_ref[...].astype(F32) + three_ref[...].astype(F32)
    mean_square = (sums[:, hid : hid + 1] + sums[:, hid + 1 : hid + 2]) / D
    inv = lax.rsqrt(mean_square + 1e-05)
    gate = sums[:, :hid] * inv
    up = sums[:, PAD : PAD + hid] * inv
    out_ref[...] = (gate / (1.0 + jnp.exp(-gate)) * up).astype(BF)


def join_body(z_lo, own_ref, one_ref, two_ref, three_ref, mark_ref, out_ref):
    rows = own_ref.shape[0]
    for step, piece in enumerate((own_ref, one_ref, two_ref, three_ref)):
        out_ref[pl.ds(pl.multiple_of((z_lo[0] ^ step) * rows, rows), rows), :] = piece[...]


def part_body(x, rows_ref, *outs):
    cols = outs[0].shape[1]
    for step, out in enumerate(outs):
        out[...] = rows_ref[:, pl.ds(pl.multiple_of((x[0] ^ step) * cols, cols), cols)]


def heads_body(rows, near_ref, far_ref, out_ref):
    for copy in range(out_ref.shape[0]):
        out_ref[copy, :rows] = near_ref[:rows]
        out_ref[copy, rows:] = far_ref[:rows]


def residual_body(rows, attn_ref, tok_ref, out_ref):
    cols = attn_ref.shape[1]
    for group in range(attn_ref.shape[0] // rows):
        at = rows + (group & 1) * rows
        side = (group >> 1) * cols
        tok = tok_ref[at : at + rows, side : side + cols].astype(F32)
        total = (attn_ref[group * rows : (group + 1) * rows].astype(F32) + tok).astype(BF)
        for copy in range(out_ref.shape[0]):
            out_ref[copy, group * rows : (group + 1) * rows] = total


def fold_body(parts_ref, out_ref):
    total = parts_ref[0].astype(F32)
    for part in range(1, parts_ref.shape[0]):
        total += parts_ref[part].astype(F32)
    out_ref[...] = total.astype(out_ref.dtype)


def down_body(core, own_ref, other_ref, weight_ref, out_ref, mark_ref):
    mark_ref[...] = jnp.zeros(mark_ref.shape, mark_ref.dtype)
    half = own_ref.shape[0]
    for place, rows_ref in ((core[0], own_ref), (1 - core[0], other_ref)):
        at = pl.ds(pl.multiple_of(place * half, half), half)
        out_ref[at, :] = dot(rows_ref[...], weight_ref[...]).astype(BF)


def gate_up(gathered, gain, gate_t, up_t, core, *marks):
    rows = gathered.shape[0] * gathered.shape[2]
    scaled, part = call(
        gate_body, [shape((rows, gate_t.shape[1]), BF), shape((rows, PAD), BF)], gathered, gain, gate_t, *marks
    )
    outs = [shape((rows // 2, 2 * PAD), BF)] * 2 + [MARK]
    return call(
        up_body, outs, scaled, part, up_t, scalars=(core,), scratch=[pltpu.VMEM((rows, PAD), F32)]
    )


def hidden_gather(pieces, hid, mark):
    hidden = call(hidden_body, shape((pieces[0].shape[0], hid), BF), *pieces, mark, weight=LONG)
    return [hidden] + line_send([hidden] * 3)


def down_project(pieces, down_weight, z_lo, core, mark):
    quarter, hid = pieces[0].shape
    width = down_weight.shape[1]
    half = call(join_body, shape((4 * quarter, hid), BF), *pieces, mark, scalars=(z_lo,))
    return call(
        down_body, [shape((8 * quarter, width), BF), MARK], half, swap(half, "core"), down_weight,
        scalars=(core,), limit=16,
    )


def all_to_all(v, axes):
    return lax.all_to_all(v, axes, split_axis=0, concat_axis=0, tiled=True)


def shards(
    tokens,
    queries,
    new_key,
    new_value,
    key_cache,
    value_cache,
    lengths,
    group_of,
    out_weight,
    norm_gain,
    gate_weight,
    up_weight,
    down_weight,
):
    groups = 32
    rows_dev, width = tokens.shape
    rows = group_of.shape[0]
    q_cols = queries.shape[1]
    cache_len = key_cache.shape[1]
    capacity = 2
    quarter = width // 4
    own_group = lax.axis_index(GRP)
    z_lo = lax.axis_index("z_lo")
    core = lax.axis_index("core")
    place_z = lax.axis_index("z_hi")
    place_y = lax.axis_index("y")
    place_x = lax.axis_index("x")

    blocks = group_of.reshape(groups, rows_dev)
    mine = pick(blocks, own_group)
    earlier = jnp.arange(rows_dev)[:, None] > jnp.arange(rows_dev)[None, :]
    my_ranks = jnp.sum((mine[:, None] == mine[None, :]) & earlier, axis=1, dtype=jnp.int32)
    my_slots = mine * capacity + my_ranks
    selector = (jnp.arange(groups * capacity, dtype=jnp.int32)[:, None] == my_slots[None, :]).astype(BF)
    packed = jnp.concatenate([queries, new_key, new_value], axis=1)
    bucket = dot(selector, packed).astype(BF).reshape(groups, capacity, packed.shape[1])
    bucket, tokens_in = lax.optimization_barrier((bucket, tokens))
    received = lax.all_to_all(bucket, GRP, split_axis=0, concat_axis=0, tiled=True)

    flat_groups = group_of.reshape(rows)
    same = flat_groups[:, None] == flat_groups[None, :]
    index = jnp.arange(rows, dtype=jnp.int32)
    before = same & (index[:, None] > index[None, :])
    in_block = index // rows_dev
    ahead = jnp.sum(before, axis=1, dtype=jnp.int32)
    block_rank = jnp.sum(before & (in_block[:, None] == in_block[None, :]), axis=1, dtype=jnp.int32)
    slot_of = in_block * capacity + block_rank
    wanted = own_group * rows_dev + jnp.arange(rows_dev, dtype=jnp.int32)
    position = flat_groups * rows_dev + ahead
    arrival = jnp.sum(
        jnp.where(position[None, :] == wanted[:, None], slot_of[None, :], 0), axis=1, keepdims=True, dtype=jnp.int32
    )
    plane = groups // 2
    gathered_at = ((flat_groups % plane) * 2 + (flat_groups // plane ^ place_z)) * rows_dev + ahead
    halves = gathered_at.reshape(2, rows // 2, 1)
    send_pos, keep_pos = pick(halves, 1 - core), pick(halves, core)

    pieces = call(part_body, [shape((rows_dev, quarter), BF)] * 4, tokens_in, scalars=(place_x,))
    pieces = [pieces[0]] + [
        lax.ppermute(pieces[step], "x", [(i, i ^ step) for i in range(4)]) for step in (1, 2, 3)
    ]

    caches = [cache.reshape(rows_dev * cache_len, HD) for cache in (key_cache, value_cache)]
    heads = call(
        functools.partial(attend_body, rows_dev, cache_len, q_cols // HD),
        shape((3 * rows_dev, q_cols), BF),
        arrival,
        received.reshape(groups * capacity, packed.shape[1]),
        lengths.reshape(rows_dev, 1),
        *pieces,
        *caches,
        scalars=(place_x,),
    )
    far_heads = swap(heads, "z_hi")
    copies = call(
        functools.partial(heads_body, rows_dev), shape((plane, 2 * rows_dev, q_cols), BF), heads, far_heads
    )
    gathered, send_pos, keep_pos = exchange(copies, send_pos, keep_pos)
    outs = [shape((rows // 2, out_weight.shape[1]), BF)] * 2
    send, keep = call(
        project_body, outs, send_pos, keep_pos, gathered.reshape(rows, q_cols), out_weight,
    )
    (own, one, two, three), _ = line_reduce(keep, swap(send, "core"), z_lo)
    attn_out = (own.astype(F32) + one.astype(F32) + two.astype(F32) + three.astype(F32)).astype(BF)
    far = lax.ppermute(attn_out, AXES, spread_pairs(1))
    near = lax.ppermute(attn_out, AXES, spread_pairs(0))
    gain = norm_gain.reshape(1, width)
    hid = down_weight.shape[0]
    gate_t, up_t = gate_weight.T, up_weight.T
    gathered = []
    for attn, tok in ((far, far_heads), (near, heads)):
        copies = call(
            functools.partial(residual_body, rows_dev), shape((plane, rows // 8, quarter), BF), attn, tok
        )
        gathered.append(all_to_all(copies, YX).reshape(4, 4, rows // 8, quarter))
    far_send, far_keep, _ = gate_up(gathered[0], gain, gate_t, up_t, core)
    far_pieces, far_sent = line_reduce(far_keep, swap(far_send, "core"), z_lo)
    near_gathered = gathered[1]
    near_send, near_keep, near_done = gate_up(near_gathered, gain, gate_t, up_t, core, far_sent)
    far_hidden = call(hidden_body, shape((far_pieces[0].shape[0], hid), BF), *far_pieces, near_done, weight=LONG)
    near_pieces, near_sent = line_reduce(near_keep, swap(near_send, "core"), z_lo)
    far_hidden = [far_hidden] + line_send([far_hidden] * 3)
    far_down, far_done = down_project(far_hidden, down_weight, z_lo, core, near_sent)
    far_parts = all_to_all(far_down.reshape(plane, rows_dev, width), YX)
    near_hidden = hidden_gather(near_pieces, hid, far_done)
    near_down, near_done = down_project(near_hidden, down_weight, z_lo, core, far_done)
    near_parts = all_to_all(near_down.reshape(plane, rows_dev, width), YX)
    kept = lax.dynamic_slice_in_dim(pick(near_gathered, place_y), place_x * rows_dev, rows_dev, axis=1)
    kept = kept.transpose(1, 0, 2).reshape(rows_dev, width)
    far_sum = call(fold_body, shape((rows_dev, width), BF), far_parts)
    near_sum = call(fold_body, shape((rows_dev, width), F32), near_parts)
    return (kept.astype(F32) + (near_sum + swap(far_sum, "z_hi").astype(F32))).astype(BF)


def solution(mesh):
    fine = Mesh(np.asarray(mesh.devices).reshape(SIZES), AXES)
    in_specs = (
        P(GRP, TP),
        P(GRP, TP),
        P(GRP, TP),
        P(GRP, TP),
        P(GRP, None, TP),
        P(GRP, None, TP),
        P(GRP),
        P(),
        P(TP, GRP),
        P(TP),
        P(TP, GRP),
        P(TP, GRP),
        P(GRP, TP),
    )
    return jax.shard_map(shards, mesh=fine, in_specs=in_specs, out_specs=P(GRP, TP), check_vma=False)
```

```python
import functools
import math

import jax
import jax.numpy as jnp
import numpy as np
from jax import lax
from jax.experimental import pallas as pl
from jax.experimental.pallas import tpu as pltpu
from jax.sharding import Mesh
from jax.sharding import PartitionSpec as P

D = 16384
HD = 128
AXES = ("z_hi", "y", "x", "z_lo", "core")
SIZES = (2, 4, 4, 4, 2)
GRP = ("z_hi", "y", "x")
TP = ("z_lo", "core")
YX = ("y", "x")
BF = jnp.bfloat16
F32 = jnp.float32
MIB = 1 << 20
LONG = 30_000_000_000
PAD = 896


def flat(z_hi, y, x, z_lo, core):
    return (((z_hi * 4 + y) * 4 + x) * 4 + z_lo) * 2 + core


def spread_pairs(flip):
    pairs = []
    for z_hi in range(2):
        for y in range(4):
            for x in range(4):
                for z_lo in range(4):
                    for core in range(2):
                        src = flat(z_hi, y, x, z_lo, core)
                        dst = flat(core ^ flip, z_lo, x, 2 * z_hi + y // 2, y % 2)
                        pairs.append((src, dst))
    return pairs


def swap(v, axis):
    return lax.ppermute(v, axis, [(0, 1), (1, 0)])


def pick(v, index):
    return lax.dynamic_index_in_dim(v, index, 0, keepdims=False)


def exchange(copies, *others):
    copies, *others = lax.optimization_barrier((copies, *others))
    got = lax.all_to_all(copies, YX, split_axis=0, concat_axis=0, tiled=True)
    return lax.optimization_barrier((got, *others))


def call(body, out_shape, *operands, scalars=(), streamed=(), scratch=(), limit=12, weight=1):
    whole = pl.BlockSpec(memory_space=pltpu.VMEM)
    single = not isinstance(out_shape, (list, tuple))
    specs = [pl.BlockSpec(memory_space=pltpu.SMEM)] * len(scalars) + [whole] * len(operands)
    specs += [pl.BlockSpec(memory_space=pltpu.HBM)] * len(streamed)
    return pl.pallas_call(
        body,
        out_shape=out_shape,
        in_specs=specs,
        out_specs=whole if single else [whole] * len(out_shape),
        scratch_shapes=list(scratch),
        compiler_params=pltpu.CompilerParams(vmem_limit_bytes=limit * MIB),
        cost_estimate=pl.CostEstimate(flops=weight, bytes_accessed=1, transcendentals=0),
    )(*[jnp.reshape(s, (1,)).astype(jnp.int32) for s in scalars], *operands, *streamed)


def shape(dims, dtype):
    return jax.ShapeDtypeStruct(dims, dtype)


def dot(a, b):
    return jnp.dot(a, b, preferred_element_type=F32)


def dot_t(a, b):
    return lax.dot_general(a, b, (((1,), (1,)), ((), ())), preferred_element_type=F32)


def attend_body(
    rows, cache_len, heads, place_x, slot_ref, got_ref, len_ref, own_tok, one_tok, two_tok, three_tok,
    key_ref, value_ref, out_ref, tok_ref,
):
    cols = own_tok.shape[1]
    for step, piece in enumerate((own_tok, one_tok, two_tok, three_tok)):
        group = place_x[0] ^ step
        at = pl.ds(pl.multiple_of((group & 1) * rows, rows), rows)
        tok_ref[at, pl.ds(pl.multiple_of((group >> 1) * cols, cols), cols)] = piece[...]
    slots = lax.broadcasted_iota(jnp.int32, (rows, got_ref.shape[0]), 1)
    compact = (slot_ref[...] == slots).astype(F32).astype(BF)
    arrived = dot(compact, got_ref[...])
    q_cols = heads * HD
    rounded = arrived[:, :q_cols].astype(BF)
    tall = jnp.concatenate([rounded[:, j * HD : (j + 1) * HD] for j in range(heads)], axis=0)
    key_new = jnp.concatenate([arrived[:, q_cols : q_cols + HD]] * heads, axis=0)
    value_new = jnp.concatenate([arrived[:, q_cols + HD :]] * heads, axis=0)
    scale = 1.0 / math.sqrt(HD)
    own = jnp.sum(tall.astype(F32) * key_new, axis=1, keepdims=True) * scale
    scores = dot_t(tall, key_ref[...]) * scale
    spot = lax.broadcasted_iota(jnp.int32, scores.shape, 1)
    row = lax.rem(lax.broadcasted_iota(jnp.int32, scores.shape, 0), rows)
    start = row * cache_len
    lens = jnp.concatenate([len_ref[...]] * heads, axis=0)
    live = (spot >= start) & (spot < start + lens)
    masked = jnp.where(live, scores, -1e30)
    top = jnp.maximum(jnp.max(masked, axis=1, keepdims=True), own)
    exp_live = jnp.where(live, jnp.exp(masked - top), 0.0)
    exp_own = jnp.exp(own - top)
    total = jnp.sum(exp_live, axis=1, keepdims=True) + exp_own
    weights = (exp_live / total).astype(BF)
    own_weight = (exp_own / total).astype(BF).astype(F32)
    out = (dot(weights, value_ref[...]) + own_weight * value_new).astype(BF)
    for j in range(heads):
        out_ref[:, j * HD : (j + 1) * HD] = out[j * rows : (j + 1) * rows]


def project_body(send_pos, keep_pos, heads_ref, weight_ref, send_ref, keep_ref):
    product = dot(heads_ref[...], weight_ref[...]).astype(BF)
    for pos, out in ((send_pos, send_ref), (keep_pos, keep_ref)):
        spot = lax.broadcasted_iota(jnp.int32, (pos.shape[0], product.shape[0]), 1)
        unsort = (pos[...] == spot).astype(F32).astype(BF)
        out[...] = dot(unsort, product).astype(BF)


def split_body(z_lo, keep_ref, got_ref, own_ref, one_ref, two_ref, three_ref, mark_ref):
    rows = own_ref.shape[0]
    mark_ref[...] = jnp.zeros(mark_ref.shape, mark_ref.dtype)
    for step, out in enumerate((own_ref, one_ref, two_ref, three_ref)):
        at = pl.ds(pl.multiple_of((z_lo[0] ^ step) * rows, rows), rows)
        out[...] = (keep_ref[at, :].astype(F32) + got_ref[at, :].astype(F32)).astype(out.dtype)


MARK = jax.ShapeDtypeStruct((8, 128), F32)


def line_reduce(keep, got, z_lo):
    rows, cols = keep.shape[0] // 4, keep.shape[1]
    outs = [shape((rows, cols), BF)] * 4 + [MARK]
    own, *pieces, mark = call(split_body, outs, keep, got, scalars=(z_lo,))
    return [own] + line_send(pieces), mark


def line_send(pieces):
    return [
        lax.ppermute(piece, "z_lo", [(i, i ^ step) for i in range(4)])
        for step, piece in zip((1, 2, 3), pieces)
    ]


def gate_body(rows_ref, gain_ref, gate_ref, *refs):
    scaled_ref, part_ref = refs[-2:]
    hid = gate_ref.shape[0]
    planes, blocks, count, cols = rows_ref.shape
    rows = planes * count
    squares = jnp.zeros((rows, 1), F32)
    for b in range(blocks):
        wide = rows_ref[:, b].reshape(rows, cols).astype(F32)
        squares += jnp.sum(wide * wide, axis=1, keepdims=True)
        at = slice(b * cols, (b + 1) * cols)
        scaled_ref[:, at] = (wide * gain_ref[:, at].astype(F32)).astype(BF)
    part_ref[:, :hid] = dot_t(scaled_ref[...], gate_ref[...]).astype(BF)
    high = squares.astype(BF).astype(F32)
    lane = lax.broadcasted_iota(jnp.int32, (rows, PAD - hid), 1)
    part_ref[:, hid:] = jnp.where(lane == 0, high, jnp.where(lane == 1, squares - high, 0.0)).astype(BF)


def up_body(core, scaled_ref, part_ref, up_ref, send_ref, keep_ref, mark_ref, total):
    mark_ref[...] = jnp.zeros(mark_ref.shape, mark_ref.dtype)
    rows, hid = scaled_ref.shape[0], up_ref.shape[0]
    half = rows // 2
    total[:, :hid] = dot_t(scaled_ref[...], up_ref[...])
    total[:, hid:] = jnp.zeros((rows, PAD - hid), F32)
    for place, out in ((1 - core[0], send_ref), (core[0], keep_ref)):
        at = pl.ds(pl.multiple_of(place * half, half), half)
        out[:, :PAD] = part_ref[at, :]
        out[:, PAD:] = total[at, :].astype(BF)


def hidden_body(own_ref, one_ref, two_ref, three_ref, mark_ref, out_ref):
    hid = out_ref.shape[1]
    sums = own_ref[...].astype(F32) + one_ref[...].astype(F32) + two_ref[...].astype(F32) + three_ref[...].astype(F32)
    mean_square = (sums[:, hid : hid + 1] + sums[:, hid + 1 : hid + 2]) / D
    inv = lax.rsqrt(mean_square + 1e-05)
    gate = sums[:, :hid] * inv
    up = sums[:, PAD : PAD + hid] * inv
    out_ref[...] = (gate / (1.0 + jnp.exp(-gate)) * up).astype(BF)


def join_body(z_lo, own_ref, one_ref, two_ref, three_ref, mark_ref, out_ref):
    rows = own_ref.shape[0]
    for step, piece in enumerate((own_ref, one_ref, two_ref, three_ref)):
        out_ref[pl.ds(pl.multiple_of((z_lo[0] ^ step) * rows, rows), rows), :] = piece[...]


def part_body(x, rows_ref, *outs):
    cols = outs[0].shape[1]
    for step, out in enumerate(outs):
        out[...] = rows_ref[:, pl.ds(pl.multiple_of((x[0] ^ step) * cols, cols), cols)]


def heads_body(rows, near_ref, far_ref, out_ref):
    for copy in range(out_ref.shape[0]):
        out_ref[copy, :rows] = near_ref[:rows]
        out_ref[copy, rows:] = far_ref[:rows]


def residual_body(rows, attn_ref, tok_ref, out_ref):
    cols = attn_ref.shape[1]
    for group in range(attn_ref.shape[0] // rows):
        at = (group & 1) * rows
        side = (group >> 1) * cols
        tok = tok_ref[at : at + rows, side : side + cols].astype(F32)
        total = (attn_ref[group * rows : (group + 1) * rows].astype(F32) + tok).astype(BF)
        for copy in range(out_ref.shape[0]):
            out_ref[copy, group * rows : (group + 1) * rows] = total


def fold_body(parts_ref, out_ref):
    total = parts_ref[0].astype(F32)
    for part in range(1, parts_ref.shape[0]):
        total += parts_ref[part].astype(F32)
    out_ref[...] = total.astype(out_ref.dtype)


def down_body(core, own_ref, other_ref, weight_ref, out_ref, mark_ref):
    mark_ref[...] = jnp.zeros(mark_ref.shape, mark_ref.dtype)
    half = own_ref.shape[0]
    for place, rows_ref in ((core[0], own_ref), (1 - core[0], other_ref)):
        at = pl.ds(pl.multiple_of(place * half, half), half)
        out_ref[at, :] = dot(rows_ref[...], weight_ref[...]).astype(BF)


def gate_up(gathered, gain, gate_t, up_t, core, *marks):
    rows = gathered.shape[0] * gathered.shape[2]
    scaled, part = call(
        gate_body, [shape((rows, gate_t.shape[1]), BF), shape((rows, PAD), BF)], gathered, gain, gate_t, *marks
    )
    outs = [shape((rows // 2, 2 * PAD), BF)] * 2 + [MARK]
    return call(
        up_body, outs, scaled, part, up_t, scalars=(core,), scratch=[pltpu.VMEM((rows, PAD), F32)]
    )


def hidden_gather(pieces, hid, mark):
    hidden = call(hidden_body, shape((pieces[0].shape[0], hid), BF), *pieces, mark, weight=LONG)
    return [hidden] + line_send([hidden] * 3)


def down_project(pieces, down_weight, z_lo, core, mark):
    quarter, hid = pieces[0].shape
    width = down_weight.shape[1]
    half = call(join_body, shape((4 * quarter, hid), BF), *pieces, mark, scalars=(z_lo,))
    return call(
        down_body, [shape((8 * quarter, width), BF), MARK], half, swap(half, "core"), down_weight,
        scalars=(core,), limit=16,
    )


def all_to_all(v, axes):
    return lax.all_to_all(v, axes, split_axis=0, concat_axis=0, tiled=True)


def shards(
    tokens,
    queries,
    new_key,
    new_value,
    key_cache,
    value_cache,
    lengths,
    group_of,
    out_weight,
    norm_gain,
    gate_weight,
    up_weight,
    down_weight,
):
    groups = 32
    rows_dev, width = tokens.shape
    rows = group_of.shape[0]
    q_cols = queries.shape[1]
    cache_len = key_cache.shape[1]
    capacity = 2
    quarter = width // 4
    own_group = lax.axis_index(GRP)
    z_lo = lax.axis_index("z_lo")
    core = lax.axis_index("core")
    place_z = lax.axis_index("z_hi")
    place_y = lax.axis_index("y")
    place_x = lax.axis_index("x")

    blocks = group_of.reshape(groups, rows_dev)
    mine = pick(blocks, own_group)
    earlier = jnp.arange(rows_dev)[:, None] > jnp.arange(rows_dev)[None, :]
    my_ranks = jnp.sum((mine[:, None] == mine[None, :]) & earlier, axis=1, dtype=jnp.int32)
    my_slots = mine * capacity + my_ranks
    selector = (jnp.arange(groups * capacity, dtype=jnp.int32)[:, None] == my_slots[None, :]).astype(BF)
    packed = jnp.concatenate([queries, new_key, new_value], axis=1)
    bucket = dot(selector, packed).astype(BF).reshape(groups, capacity, packed.shape[1])
    bucket, tokens_in = lax.optimization_barrier((bucket, tokens))
    received = lax.all_to_all(bucket, GRP, split_axis=0, concat_axis=0, tiled=True)

    flat_groups = group_of.reshape(rows)
    same = flat_groups[:, None] == flat_groups[None, :]
    index = jnp.arange(rows, dtype=jnp.int32)
    before = same & (index[:, None] > index[None, :])
    in_block = index // rows_dev
    ahead = jnp.sum(before, axis=1, dtype=jnp.int32)
    block_rank = jnp.sum(before & (in_block[:, None] == in_block[None, :]), axis=1, dtype=jnp.int32)
    slot_of = in_block * capacity + block_rank
    wanted = own_group * rows_dev + jnp.arange(rows_dev, dtype=jnp.int32)
    position = flat_groups * rows_dev + ahead
    arrival = jnp.sum(
        jnp.where(position[None, :] == wanted[:, None], slot_of[None, :], 0), axis=1, keepdims=True, dtype=jnp.int32
    )
    plane = groups // 2
    gathered_at = ((flat_groups % plane) * 2 + (flat_groups // plane ^ place_z)) * rows_dev + ahead
    halves = gathered_at.reshape(2, rows // 2, 1)
    send_pos, keep_pos = pick(halves, 1 - core), pick(halves, core)

    pieces = call(part_body, [shape((rows_dev, quarter), BF)] * 4, tokens_in, scalars=(place_x,))
    pieces = [pieces[0]] + [
        lax.ppermute(pieces[step], "x", [(i, i ^ step) for i in range(4)]) for step in (1, 2, 3)
    ]

    caches = [cache.reshape(rows_dev * cache_len, HD) for cache in (key_cache, value_cache)]
    heads, near_tok = call(
        functools.partial(attend_body, rows_dev, cache_len, q_cols // HD),
        [shape((rows_dev, q_cols), BF), shape((2 * rows_dev, q_cols), BF)],
        arrival,
        received.reshape(groups * capacity, packed.shape[1]),
        lengths.reshape(rows_dev, 1),
        *pieces,
        *caches,
        scalars=(place_x,),
    )
    far_heads, far_tok = swap(heads, "z_hi"), swap(near_tok, "z_hi")
    copies = call(
        functools.partial(heads_body, rows_dev), shape((plane, 2 * rows_dev, q_cols), BF), heads, far_heads
    )
    gathered, send_pos, keep_pos = exchange(copies, send_pos, keep_pos)
    outs = [shape((rows // 2, out_weight.shape[1]), BF)] * 2
    send, keep = call(
        project_body, outs, send_pos, keep_pos, gathered.reshape(rows, q_cols), out_weight,
    )
    (own, one, two, three), _ = line_reduce(keep, swap(send, "core"), z_lo)
    attn_out = (own.astype(F32) + one.astype(F32) + two.astype(F32) + three.astype(F32)).astype(BF)
    far = lax.ppermute(attn_out, AXES, spread_pairs(1))
    near = lax.ppermute(attn_out, AXES, spread_pairs(0))
    gain = norm_gain.reshape(1, width)
    hid = down_weight.shape[0]
    gate_t, up_t = gate_weight.T, up_weight.T
    gathered = []
    for attn, tok in ((far, far_tok), (near, near_tok)):
        copies = call(
            functools.partial(residual_body, rows_dev), shape((plane, rows // 8, quarter), BF), attn, tok
        )
        gathered.append(all_to_all(copies, YX).reshape(4, 4, rows // 8, quarter))
    far_send, far_keep, _ = gate_up(gathered[0], gain, gate_t, up_t, core)
    far_pieces, far_sent = line_reduce(far_keep, swap(far_send, "core"), z_lo)
    near_gathered = gathered[1]
    near_send, near_keep, near_done = gate_up(near_gathered, gain, gate_t, up_t, core, far_sent)
    far_hidden = call(hidden_body, shape((far_pieces[0].shape[0], hid), BF), *far_pieces, near_done, weight=LONG)
    near_pieces, near_sent = line_reduce(near_keep, swap(near_send, "core"), z_lo)
    far_hidden = [far_hidden] + line_send([far_hidden] * 3)
    far_down, far_done = down_project(far_hidden, down_weight, z_lo, core, near_sent)
    far_parts = all_to_all(far_down.reshape(plane, rows_dev, width), YX)
    near_hidden = hidden_gather(near_pieces, hid, far_done)
    near_down, near_done = down_project(near_hidden, down_weight, z_lo, core, far_done)
    near_parts = all_to_all(near_down.reshape(plane, rows_dev, width), YX)
    kept = lax.dynamic_slice_in_dim(pick(near_gathered, place_y), place_x * rows_dev, rows_dev, axis=1)
    kept = kept.transpose(1, 0, 2).reshape(rows_dev, width)
    far_sum = call(fold_body, shape((rows_dev, width), BF), far_parts)
    near_sum = call(fold_body, shape((rows_dev, width), F32), near_parts)
    return (kept.astype(F32) + (near_sum + swap(far_sum, "z_hi").astype(F32))).astype(BF)


def solution(mesh):
    fine = Mesh(np.asarray(mesh.devices).reshape(SIZES), AXES)
    in_specs = (
        P(GRP, TP),
        P(GRP, TP),
        P(GRP, TP),
        P(GRP, TP),
        P(GRP, None, TP),
        P(GRP, None, TP),
        P(GRP),
        P(),
        P(TP, GRP),
        P(TP),
        P(TP, GRP),
        P(TP, GRP),
        P(GRP, TP),
    )
    return jax.shard_map(shards, mesh=fine, in_specs=in_specs, out_specs=P(GRP, TP), check_vma=False)
```

```python
import functools
import math

import jax
import jax.numpy as jnp
import numpy as np
from jax import lax
from jax.experimental import pallas as pl
from jax.experimental.pallas import tpu as pltpu
from jax.sharding import Mesh
from jax.sharding import PartitionSpec as P

D = 16384
HD = 128
AXES = ("z_hi", "y", "x", "z_lo", "core")
SIZES = (2, 4, 4, 4, 2)
GRP = ("z_hi", "y", "x")
TP = ("z_lo", "core")
YX = ("y", "x")
BF = jnp.bfloat16
F32 = jnp.float32
MIB = 1 << 20
LONG = 30_000_000_000
PAD = 896


def flat(z_hi, y, x, z_lo, core):
    return (((z_hi * 4 + y) * 4 + x) * 4 + z_lo) * 2 + core


def spread_pairs(flip):
    pairs = []
    for z_hi in range(2):
        for y in range(4):
            for x in range(4):
                for z_lo in range(4):
                    for core in range(2):
                        src = flat(z_hi, y, x, z_lo, core)
                        dst = flat(core ^ flip, z_lo, x, 2 * z_hi + y // 2, y % 2)
                        pairs.append((src, dst))
    return pairs


def swap(v, axis):
    return lax.ppermute(v, axis, [(0, 1), (1, 0)])


def pick(v, index):
    return lax.dynamic_index_in_dim(v, index, 0, keepdims=False)


def exchange(copies, *others):
    copies, *others = lax.optimization_barrier((copies, *others))
    got = lax.all_to_all(copies, YX, split_axis=0, concat_axis=0, tiled=True)
    return lax.optimization_barrier((got, *others))


def call(body, out_shape, *operands, scalars=(), streamed=(), scratch=(), limit=12, weight=1):
    whole = pl.BlockSpec(memory_space=pltpu.VMEM)
    single = not isinstance(out_shape, (list, tuple))
    specs = [pl.BlockSpec(memory_space=pltpu.SMEM)] * len(scalars) + [whole] * len(operands)
    specs += [pl.BlockSpec(memory_space=pltpu.HBM)] * len(streamed)
    return pl.pallas_call(
        body,
        out_shape=out_shape,
        in_specs=specs,
        out_specs=whole if single else [whole] * len(out_shape),
        scratch_shapes=list(scratch),
        compiler_params=pltpu.CompilerParams(vmem_limit_bytes=limit * MIB),
        cost_estimate=pl.CostEstimate(flops=weight, bytes_accessed=1, transcendentals=0),
    )(*[jnp.reshape(s, (1,)).astype(jnp.int32) for s in scalars], *operands, *streamed)


def shape(dims, dtype):
    return jax.ShapeDtypeStruct(dims, dtype)


def dot(a, b):
    return jnp.dot(a, b, preferred_element_type=F32)


def dot_t(a, b):
    return lax.dot_general(a, b, (((1,), (1,)), ((), ())), preferred_element_type=F32)


def as_column(row_ref):
    sizes = (row_ref.shape[1],) * 2
    same = lax.broadcasted_iota(jnp.int32, sizes, 0) == lax.broadcasted_iota(jnp.int32, sizes, 1)
    return jnp.sum(jnp.where(same, row_ref[...], 0), axis=1, keepdims=True)


def attend_body(
    rows, cache_len, heads, place_x, slot_ref, got_ref, len_ref, own_tok, one_tok, two_tok, three_tok,
    key_ref, value_ref, out_ref, tok_ref,
):
    cols = own_tok.shape[1]
    for step, piece in enumerate((own_tok, one_tok, two_tok, three_tok)):
        group = place_x[0] ^ step
        at = pl.ds(pl.multiple_of((group & 1) * rows, rows), rows)
        tok_ref[at, pl.ds(pl.multiple_of((group >> 1) * cols, cols), cols)] = piece[...]
    slots = lax.broadcasted_iota(jnp.int32, (rows, got_ref.shape[0]), 1)
    compact = (as_column(slot_ref) == slots).astype(F32).astype(BF)
    arrived = dot(compact, got_ref[...])
    q_cols = heads * HD
    rounded = arrived[:, :q_cols].astype(BF)
    tall = jnp.concatenate([rounded[:, j * HD : (j + 1) * HD] for j in range(heads)], axis=0)
    key_new = jnp.concatenate([arrived[:, q_cols : q_cols + HD]] * heads, axis=0)
    value_new = jnp.concatenate([arrived[:, q_cols + HD :]] * heads, axis=0)
    scale = 1.0 / math.sqrt(HD)
    own = jnp.sum(tall.astype(F32) * key_new, axis=1, keepdims=True) * scale
    scores = dot_t(tall, key_ref[...]) * scale
    spot = lax.broadcasted_iota(jnp.int32, scores.shape, 1)
    row = lax.rem(lax.broadcasted_iota(jnp.int32, scores.shape, 0), rows)
    start = row * cache_len
    lens = jnp.concatenate([as_column(len_ref)] * heads, axis=0)
    live = (spot >= start) & (spot < start + lens)
    masked = jnp.where(live, scores, -1e30)
    top = jnp.maximum(jnp.max(masked, axis=1, keepdims=True), own)
    exp_live = jnp.where(live, jnp.exp(masked - top), 0.0)
    exp_own = jnp.exp(own - top)
    total = jnp.sum(exp_live, axis=1, keepdims=True) + exp_own
    weights = (exp_live / total).astype(BF)
    own_weight = (exp_own / total).astype(BF).astype(F32)
    out = (dot(weights, value_ref[...]) + own_weight * value_new).astype(BF)
    for j in range(heads):
        out_ref[:, j * HD : (j + 1) * HD] = out[j * rows : (j + 1) * rows]


def project_body(send_pos, keep_pos, heads_ref, weight_ref, send_ref, keep_ref):
    product = dot(heads_ref[...], weight_ref[...]).astype(BF)
    for pos, out in ((send_pos, send_ref), (keep_pos, keep_ref)):
        spot = lax.broadcasted_iota(jnp.int32, (pos.shape[0], product.shape[0]), 1)
        unsort = (pos[...] == spot).astype(F32).astype(BF)
        out[...] = dot(unsort, product).astype(BF)


def split_body(z_lo, keep_ref, got_ref, own_ref, one_ref, two_ref, three_ref, mark_ref):
    rows = own_ref.shape[0]
    mark_ref[...] = jnp.zeros(mark_ref.shape, mark_ref.dtype)
    for step, out in enumerate((own_ref, one_ref, two_ref, three_ref)):
        at = pl.ds(pl.multiple_of((z_lo[0] ^ step) * rows, rows), rows)
        out[...] = (keep_ref[at, :].astype(F32) + got_ref[at, :].astype(F32)).astype(out.dtype)


MARK = jax.ShapeDtypeStruct((8, 128), F32)


def line_reduce(keep, got, z_lo):
    rows, cols = keep.shape[0] // 4, keep.shape[1]
    outs = [shape((rows, cols), BF)] * 4 + [MARK]
    own, *pieces, mark = call(split_body, outs, keep, got, scalars=(z_lo,))
    return [own] + line_send(pieces), mark


def line_send(pieces):
    return [
        lax.ppermute(piece, "z_lo", [(i, i ^ step) for i in range(4)])
        for step, piece in zip((1, 2, 3), pieces)
    ]


def gate_body(rows_ref, gain_ref, gate_ref, *refs):
    scaled_ref, part_ref = refs[-2:]
    hid = gate_ref.shape[0]
    planes, blocks, count, cols = rows_ref.shape
    rows = planes * count
    squares = jnp.zeros((rows, 1), F32)
    for b in range(blocks):
        wide = rows_ref[:, b].reshape(rows, cols).astype(F32)
        squares += jnp.sum(wide * wide, axis=1, keepdims=True)
        at = slice(b * cols, (b + 1) * cols)
        scaled_ref[:, at] = (wide * gain_ref[:, at].astype(F32)).astype(BF)
    part_ref[:, :hid] = dot_t(scaled_ref[...], gate_ref[...]).astype(BF)
    high = squares.astype(BF).astype(F32)
    lane = lax.broadcasted_iota(jnp.int32, (rows, PAD - hid), 1)
    part_ref[:, hid:] = jnp.where(lane == 0, high, jnp.where(lane == 1, squares - high, 0.0)).astype(BF)


def up_body(core, scaled_ref, part_ref, up_ref, send_ref, keep_ref, mark_ref, total):
    mark_ref[...] = jnp.zeros(mark_ref.shape, mark_ref.dtype)
    rows, hid = scaled_ref.shape[0], up_ref.shape[0]
    half = rows // 2
    total[:, :hid] = dot_t(scaled_ref[...], up_ref[...])
    total[:, hid:] = jnp.zeros((rows, PAD - hid), F32)
    for place, out in ((1 - core[0], send_ref), (core[0], keep_ref)):
        at = pl.ds(pl.multiple_of(place * half, half), half)
        out[:, :PAD] = part_ref[at, :]
        out[:, PAD:] = total[at, :].astype(BF)


def hidden_body(own_ref, one_ref, two_ref, three_ref, mark_ref, out_ref):
    hid = out_ref.shape[1]
    sums = own_ref[...].astype(F32) + one_ref[...].astype(F32) + two_ref[...].astype(F32) + three_ref[...].astype(F32)
    mean_square = (sums[:, hid : hid + 1] + sums[:, hid + 1 : hid + 2]) / D
    inv = lax.rsqrt(mean_square + 1e-05)
    gate = sums[:, :hid] * inv
    up = sums[:, PAD : PAD + hid] * inv
    out_ref[...] = (gate / (1.0 + jnp.exp(-gate)) * up).astype(BF)


def join_body(z_lo, own_ref, one_ref, two_ref, three_ref, mark_ref, out_ref):
    rows = own_ref.shape[0]
    for step, piece in enumerate((own_ref, one_ref, two_ref, three_ref)):
        out_ref[pl.ds(pl.multiple_of((z_lo[0] ^ step) * rows, rows), rows), :] = piece[...]


def part_body(x, rows_ref, *outs):
    cols = outs[0].shape[1]
    for step, out in enumerate(outs):
        out[...] = rows_ref[:, pl.ds(pl.multiple_of((x[0] ^ step) * cols, cols), cols)]


def heads_body(rows, near_ref, far_ref, out_ref):
    for copy in range(out_ref.shape[0]):
        out_ref[copy, :rows] = near_ref[:rows]
        out_ref[copy, rows:] = far_ref[:rows]


def residual_body(rows, attn_ref, tok_ref, out_ref):
    cols = attn_ref.shape[1]
    for group in range(attn_ref.shape[0] // rows):
        at = (group & 1) * rows
        side = (group >> 1) * cols
        tok = tok_ref[at : at + rows, side : side + cols].astype(F32)
        total = (attn_ref[group * rows : (group + 1) * rows].astype(F32) + tok).astype(BF)
        for copy in range(out_ref.shape[0]):
            out_ref[copy, group * rows : (group + 1) * rows] = total


def fold_body(parts_ref, out_ref):
    total = parts_ref[0].astype(F32)
    for part in range(1, parts_ref.shape[0]):
        total += parts_ref[part].astype(F32)
    out_ref[...] = total.astype(out_ref.dtype)


def down_body(core, own_ref, other_ref, weight_ref, out_ref, mark_ref):
    mark_ref[...] = jnp.zeros(mark_ref.shape, mark_ref.dtype)
    half = own_ref.shape[0]
    for place, rows_ref in ((core[0], own_ref), (1 - core[0], other_ref)):
        at = pl.ds(pl.multiple_of(place * half, half), half)
        out_ref[at, :] = dot(rows_ref[...], weight_ref[...]).astype(BF)


def gate_up(gathered, gain, gate_t, up_t, core, *marks):
    rows = gathered.shape[0] * gathered.shape[2]
    scaled, part = call(
        gate_body, [shape((rows, gate_t.shape[1]), BF), shape((rows, PAD), BF)], gathered, gain, gate_t, *marks
    )
    outs = [shape((rows // 2, 2 * PAD), BF)] * 2 + [MARK]
    return call(
        up_body, outs, scaled, part, up_t, scalars=(core,), scratch=[pltpu.VMEM((rows, PAD), F32)]
    )


def hidden_gather(pieces, hid, mark):
    hidden = call(hidden_body, shape((pieces[0].shape[0], hid), BF), *pieces, mark, weight=LONG)
    return [hidden] + line_send([hidden] * 3)


def down_project(pieces, down_weight, z_lo, core, mark):
    quarter, hid = pieces[0].shape
    width = down_weight.shape[1]
    half = call(join_body, shape((4 * quarter, hid), BF), *pieces, mark, scalars=(z_lo,))
    return call(
        down_body, [shape((8 * quarter, width), BF), MARK], half, swap(half, "core"), down_weight,
        scalars=(core,), limit=16,
    )


def all_to_all(v, axes):
    return lax.all_to_all(v, axes, split_axis=0, concat_axis=0, tiled=True)


def shards(
    tokens,
    queries,
    new_key,
    new_value,
    key_cache,
    value_cache,
    lengths,
    group_of,
    out_weight,
    norm_gain,
    gate_weight,
    up_weight,
    down_weight,
):
    groups = 32
    rows_dev, width = tokens.shape
    rows = group_of.shape[0]
    q_cols = queries.shape[1]
    cache_len = key_cache.shape[1]
    capacity = 2
    quarter = width // 4
    own_group = lax.axis_index(GRP)
    z_lo = lax.axis_index("z_lo")
    core = lax.axis_index("core")
    place_z = lax.axis_index("z_hi")
    place_y = lax.axis_index("y")
    place_x = lax.axis_index("x")

    blocks = group_of.reshape(groups, rows_dev)
    mine = pick(blocks, own_group)
    earlier = jnp.arange(rows_dev)[:, None] > jnp.arange(rows_dev)[None, :]
    my_ranks = jnp.sum((mine[:, None] == mine[None, :]) & earlier, axis=1, dtype=jnp.int32)
    my_slots = mine * capacity + my_ranks
    selector = (jnp.arange(groups * capacity, dtype=jnp.int32)[:, None] == my_slots[None, :]).astype(BF)
    packed = jnp.concatenate([queries, new_key, new_value], axis=1)
    bucket = dot(selector, packed).astype(BF).reshape(groups, capacity, packed.shape[1])
    bucket, tokens_in = lax.optimization_barrier((bucket, tokens))
    received = lax.all_to_all(bucket, GRP, split_axis=0, concat_axis=0, tiled=True)

    flat_groups = group_of.reshape(rows)
    same = flat_groups[:, None] == flat_groups[None, :]
    index = jnp.arange(rows, dtype=jnp.int32)
    before = same & (index[:, None] > index[None, :])
    in_block = index // rows_dev
    ahead = jnp.sum(before, axis=1, dtype=jnp.int32)
    block_rank = jnp.sum(before & (in_block[:, None] == in_block[None, :]), axis=1, dtype=jnp.int32)
    slot_of = in_block * capacity + block_rank
    wanted = own_group * rows_dev + jnp.arange(rows_dev, dtype=jnp.int32)
    position = flat_groups * rows_dev + ahead
    arrival = jnp.sum(
        jnp.where(position[None, :] == wanted[:, None], slot_of[None, :], 0), axis=1, dtype=jnp.int32
    )[None, :]
    plane = groups // 2
    gathered_at = ((flat_groups % plane) * 2 + (flat_groups // plane ^ place_z)) * rows_dev + ahead
    halves = gathered_at.reshape(2, rows // 2, 1)
    send_pos, keep_pos = pick(halves, 1 - core), pick(halves, core)

    pieces = call(part_body, [shape((rows_dev, quarter), BF)] * 4, tokens_in, scalars=(place_x,))
    pieces = [pieces[0]] + [
        lax.ppermute(pieces[step], "x", [(i, i ^ step) for i in range(4)]) for step in (1, 2, 3)
    ]

    caches = [cache.reshape(rows_dev * cache_len, HD) for cache in (key_cache, value_cache)]
    heads, near_tok = call(
        functools.partial(attend_body, rows_dev, cache_len, q_cols // HD),
        [shape((rows_dev, q_cols), BF), shape((2 * rows_dev, q_cols), BF)],
        arrival,
        received.reshape(groups * capacity, packed.shape[1]),
        lengths.reshape(1, rows_dev),
        *pieces,
        *caches,
        scalars=(place_x,),
    )
    far_heads, far_tok = swap(heads, "z_hi"), swap(near_tok, "z_hi")
    copies = call(
        functools.partial(heads_body, rows_dev), shape((plane, 2 * rows_dev, q_cols), BF), heads, far_heads
    )
    gathered, send_pos, keep_pos = exchange(copies, send_pos, keep_pos)
    outs = [shape((rows // 2, out_weight.shape[1]), BF)] * 2
    send, keep = call(
        project_body, outs, send_pos, keep_pos, gathered.reshape(rows, q_cols), out_weight,
    )
    (own, one, two, three), _ = line_reduce(keep, swap(send, "core"), z_lo)
    attn_out = (own.astype(F32) + one.astype(F32) + two.astype(F32) + three.astype(F32)).astype(BF)
    far = lax.ppermute(attn_out, AXES, spread_pairs(1))
    near = lax.ppermute(attn_out, AXES, spread_pairs(0))
    gain = norm_gain.reshape(1, width)
    hid = down_weight.shape[0]
    gate_t, up_t = gate_weight.T, up_weight.T
    gathered = []
    for attn, tok in ((far, far_tok), (near, near_tok)):
        copies = call(
            functools.partial(residual_body, rows_dev), shape((plane, rows // 8, quarter), BF), attn, tok
        )
        gathered.append(all_to_all(copies, YX).reshape(4, 4, rows // 8, quarter))
    far_send, far_keep, _ = gate_up(gathered[0], gain, gate_t, up_t, core)
    far_pieces, far_sent = line_reduce(far_keep, swap(far_send, "core"), z_lo)
    near_gathered = gathered[1]
    near_send, near_keep, near_done = gate_up(near_gathered, gain, gate_t, up_t, core, far_sent)
    far_hidden = call(hidden_body, shape((far_pieces[0].shape[0], hid), BF), *far_pieces, near_done, weight=LONG)
    near_pieces, near_sent = line_reduce(near_keep, swap(near_send, "core"), z_lo)
    far_hidden = [far_hidden] + line_send([far_hidden] * 3)
    far_down, far_done = down_project(far_hidden, down_weight, z_lo, core, near_sent)
    far_parts = all_to_all(far_down.reshape(plane, rows_dev, width), YX)
    near_hidden = hidden_gather(near_pieces, hid, far_done)
    near_down, near_done = down_project(near_hidden, down_weight, z_lo, core, far_done)
    near_parts = all_to_all(near_down.reshape(plane, rows_dev, width), YX)
    kept = lax.dynamic_slice_in_dim(pick(near_gathered, place_y), place_x * rows_dev, rows_dev, axis=1)
    kept = kept.transpose(1, 0, 2).reshape(rows_dev, width)
    far_sum = call(fold_body, shape((rows_dev, width), BF), far_parts)
    near_sum = call(fold_body, shape((rows_dev, width), F32), near_parts)
    return (kept.astype(F32) + (near_sum + swap(far_sum, "z_hi").astype(F32))).astype(BF)


def solution(mesh):
    fine = Mesh(np.asarray(mesh.devices).reshape(SIZES), AXES)
    in_specs = (
        P(GRP, TP),
        P(GRP, TP),
        P(GRP, TP),
        P(GRP, TP),
        P(GRP, None, TP),
        P(GRP, None, TP),
        P(GRP),
        P(),
        P(TP, GRP),
        P(TP),
        P(TP, GRP),
        P(TP, GRP),
        P(GRP, TP),
    )
    return jax.shard_map(shards, mesh=fine, in_specs=in_specs, out_specs=P(GRP, TP), check_vma=False)
```
